128 devices in a mesh: prompt: 4 (over z), comp: 32 (over x, y, core).
Axes of the slice: x: 4, y: 4, z: 4, core: 2. Of those that a mesh axis runs over, the one named last changes fastest.
Arguments:
- x_in: bfloat16 [32768, 8192], P(('prompt', 'comp')), may hold values from -6 to 6
- b_in: bfloat16 [32768, 128], P(('prompt', 'comp')), may hold values from -6 to 6
- c_in: bfloat16 [32768, 128], P(('prompt', 'comp')), may hold values from -0.5 to 0.5
- dt_raw: float32 [32768, 128], P(('prompt', 'comp')), may hold values from -6 to 6
- dy_up: bfloat16 [32768, 8192], P(('prompt', 'comp')), may hold values from -6 to 6
- advantages: int32 [32768], P(('prompt', 'comp')), may hold values from -4096 to 4096
- lengths: int32 [128], P(('prompt', 'comp')), may hold values from 64 to 256
- prompt_of: int32 [128, 1], replicated, may hold values from 0 to 3
- a_log: float32 [128], replicated, may hold values from -6.2 to -3
- dt_bias: float32 [128], replicated, may hold values from -1 to 1
- skip_gain: float32 [128], replicated, may hold values from 0.5 to 1.5
- conv_w: float32 [4, 8192], replicated, may hold values from -3 to 3
- conv_b: float32 [8192], replicated, may hold values from -3 to 3
- prompt_state: float32 [4, 128, 64, 128], P('prompt', 'comp'), may hold values from -6 to 6
- prompt_tail: bfloat16 [4, 3, 8192], P('prompt', None, 'comp'), may hold values from -6 to 6
Outputs:
- scores: float32 [32768], P(('prompt', 'comp'))
- grad_x: bfloat16 [32768, 8192], P(('prompt', 'comp'))
- grad_state: float32 [4, 128, 64, 128], P('prompt', 'comp')
- grad_tail: float32 [4, 3, 8192], P('prompt', None, 'comp')
The draws below stay inside these ranges and needn't reach their ends.
Inputs may be any that keep to these rules, and one draw needn't show every extreme that they name: `prompt_of`: every one of the 4 prompts has at least one slice.
All inputs are finite; a program needn't handle non-finite values.
Results may differ from the reference program's by a relative error of at most 0.002.
Values may be sent and summed in bfloat16 or wider, within the bound.
A program may use at most 256 MiB of HBM per device.

```python
import jax
import jax.numpy as jnp
from jax import lax

HEADS = 128
HEAD_DIM = 64
STATE = 128
CONV = 4
TOK_DEV = 256
PROMPTS = 4
SLICES = 128
TOKENS = 32768
DEVICES = 128


def touch_ends(array, stream_key, low, high):
    shape = array.shape
    place = [jax.random.randint(jax.random.fold_in(stream_key, axis), (), 0, shape[axis]) for axis in range(len(shape))]
    array = array.at[tuple(place)].set(low)
    longest = shape.index(max(shape))
    place[longest] = (place[longest] + 1) % shape[longest]
    return array.at[tuple(place)].set(high)


def shard_levels(own_key, extent, cuts, smallest, top_value):
    factor_of = 1.0
    for position, shards_of in cuts:
        steps = jax.random.uniform(jax.random.fold_in(jax.random.fold_in(own_key, 6), position), (shards_of,), jnp.float32, smallest / len(cuts), top_value / len(cuts))
        factor_of = factor_of * jnp.repeat(jnp.exp(steps), extent[position] // shards_of).reshape((-1,) + (1,) * (len(extent) - 1 - position))
    return factor_of


def choose_distinct(own_key, rows, amount, top, lift):
    order = jax.random.permutation(jax.random.fold_in(own_key, 1), amount)
    pull = order
    for power in range(3):
        pull = pull * pull // amount
    pull = pull * lift // amount
    lots = jax.random.randint(jax.random.fold_in(own_key, 2), (rows, amount), 0, 4096) + pull
    holders = jax.random.permutation(jax.random.fold_in(own_key, 3), rows)[jnp.arange(amount) % rows]
    lots = jnp.where(jnp.arange(rows)[:, None] == holders[None, :], 1 << 14, lots)
    priority = lots * amount + jnp.arange(amount)
    return lax.top_k(priority.astype(jnp.int32), top)[1].astype(jnp.int32)


def noise(stream_key, dims, spread, most, shards=(), held_as=jnp.bfloat16):
    loudness = shard_levels(stream_key, dims, shards, -0.22, 0.18) if shards else 1.0
    entries = jax.random.normal(stream_key, dims, jnp.float32) * spread * loudness
    return jnp.minimum(jnp.maximum(entries, -most), most).astype(held_as)


def setup_inputs(seed: int = 0) -> dict:
    splits = jax.random.split(jax.random.key(seed), 16)
    return {
        "x_in": noise(splits[0], (TOKENS, HEADS * HEAD_DIM), 1.0, 6.0, ((0, 128),)),
        "b_in": noise(splits[1], (TOKENS, STATE), 1.0, 6.0, ((0, 128),)),
        "c_in": noise(splits[2], (TOKENS, STATE), STATE ** -0.5, 0.5, ((0, 128),)),
        "dt_raw": noise(splits[3], (TOKENS, HEADS), 1.0, 6.0, ((0, 128),), jnp.float32),
        "dy_up": noise(splits[4], (TOKENS, HEADS * HEAD_DIM), 1.0, 6.0, ((0, 128),)),
        "advantages": touch_ends(jax.random.randint(splits[5], (TOKENS,), -4096, 4097), jax.random.fold_in(splits[5], 1), -4096, 4096).astype(jnp.int32),
        "lengths": touch_ends(jax.random.randint(splits[6], (SLICES,), TOK_DEV // 4, TOK_DEV + 1), jax.random.fold_in(splits[6], 1), TOK_DEV // 4, TOK_DEV).astype(jnp.int32),
        "prompt_of": choose_distinct(splits[7], SLICES, PROMPTS, 1, 2048),
        "a_log": jnp.clip(jax.random.uniform(splits[8], (HEADS,), jnp.float32, -6.2, -3.0), -6.2, -3.0),
        "dt_bias": jnp.clip(jax.random.uniform(splits[9], (HEADS,), jnp.float32, -1.0, 1.0), -1.0, 1.0),
        "skip_gain": jnp.clip(jax.random.uniform(splits[10], (HEADS,), jnp.float32, 0.5, 1.5), 0.5, 1.5),
        "conv_w": noise(splits[11], (CONV, HEADS * HEAD_DIM), CONV ** -0.5, 3.0, (), jnp.float32),
        "conv_b": noise(splits[12], (HEADS * HEAD_DIM,), 0.5, 3.0, (), jnp.float32),
        "prompt_state": noise(splits[13], (PROMPTS, HEADS, HEAD_DIM, STATE), 1.0, 6.0, ((0, 4), (1, 32)), jnp.float32),
        "prompt_tail": noise(splits[14], (PROMPTS, CONV - 1, HEADS * HEAD_DIM), 1.0, 6.0, ((0, 4), (2, 32))),
    }


def head_group(extended, prefix_state, step_size, decay_rate, skip_part, taps, bias, upstream, affinity, c_rows):
    tok_rows = step_size.shape[0]
    group_heads = step_size.shape[1]
    head_width = prefix_state.shape[1]
    conv = bias[None, :] + taps[0][None, :] * extended[0:tok_rows]
    for offset in range(1, taps.shape[0]):
        conv = conv + taps[offset][None, :] * extended[offset:offset + tok_rows]
    activated = jax.nn.silu(conv).reshape(tok_rows, group_heads, head_width)
    log_decay = -jnp.cumsum(step_size * decay_rate[None, :], axis=0)
    later_log = log_decay.T[:, :, None]
    earlier_log = log_decay.T[:, None, :]
    causal = jnp.arange(tok_rows)[:, None] >= jnp.arange(tok_rows)[None, :]
    decay_mask = jnp.where(causal[None], jnp.exp(jnp.minimum(later_log - earlier_log, 0.0)), 0.0)
    weighted = decay_mask * affinity[None]
    local_part = jnp.einsum('hts,shp->thp', weighted, activated * step_size[:, :, None], precision=lax.Precision.HIGHEST)
    prefix_part = jnp.exp(log_decay)[:, :, None] * jnp.einsum('tn,hpn->thp', c_rows, prefix_state, precision=lax.Precision.HIGHEST)
    outputs = local_part + prefix_part + skip_part[None, :, None] * activated
    return lax.optimization_barrier(jnp.sum(outputs.reshape(tok_rows, -1) * upstream, axis=1))

def local_scores(extended, prefix_state, b_rows, c_rows, dt_rows, upstream, token_weight, a_log, dt_bias, skip_gain, conv_w, conv_b):
    tok_rows = dt_rows.shape[0]
    head_count = dt_rows.shape[1]
    head_width = prefix_state.shape[1]
    tail_len = extended.shape[0] - tok_rows
    group_heads = min(16, head_count)
    group_count = head_count // group_heads
    group_width = group_heads * head_width
    c_float = c_rows.astype(jnp.float32)
    affinity = jnp.dot(c_rows, b_rows.T, preferred_element_type=jnp.float32)
    step_size = jax.nn.softplus(dt_rows + dt_bias[None, :])
    decay_rate = jnp.exp(a_log)
    ext_groups = extended.reshape(tok_rows + tail_len, group_count, group_width).transpose(1, 0, 2)
    up_groups = upstream.reshape(tok_rows, group_count, group_width).transpose(1, 0, 2)
    tap_groups = conv_w.reshape(conv_w.shape[0], group_count, group_width).transpose(1, 0, 2)
    bias_groups = conv_b.reshape(group_count, group_width)
    step_groups = step_size.reshape(tok_rows, group_count, group_heads).transpose(1, 0, 2)
    rate_groups = decay_rate.reshape(group_count, group_heads)
    skip_groups = skip_gain.reshape(group_count, group_heads)
    state_groups = prefix_state.reshape(group_count, group_heads, head_width, prefix_state.shape[2])

    def one_group(packed):
        return head_group(packed[0], packed[1], packed[2], packed[3], packed[4], packed[5], packed[6], packed[7], affinity, c_float)
    partials = lax.map(one_group, (ext_groups, state_groups, step_groups, rate_groups, skip_groups, tap_groups, bias_groups, up_groups))
    return token_weight * lax.optimization_barrier(jnp.sum(partials, axis=0))

def reference(x_in, b_in, c_in, dt_raw, dy_up, advantages, lengths, prompt_of, a_log, dt_bias, skip_gain, conv_w, conv_b, prompt_state, prompt_tail):
    tail_len = CONV - 1
    prompt_ids = jnp.arange(PROMPTS, dtype=jnp.int32)
    positions = jnp.arange(TOK_DEV, dtype=jnp.int32)

    def step(carry, slice_index):
        acc_state, acc_tail = carry
        row_start = (slice_index * TOK_DEV).astype(jnp.int32)
        x_rows = lax.dynamic_slice_in_dim(x_in, row_start, TOK_DEV, 0)
        b_rows = lax.dynamic_slice_in_dim(b_in, row_start, TOK_DEV, 0)
        c_rows = lax.dynamic_slice_in_dim(c_in, row_start, TOK_DEV, 0)
        dt_rows = lax.dynamic_slice_in_dim(dt_raw, row_start, TOK_DEV, 0)
        upstream = lax.dynamic_slice_in_dim(dy_up, row_start, TOK_DEV, 0)
        adv_rows = lax.dynamic_slice_in_dim(advantages, row_start, TOK_DEV, 0)
        live = lengths[slice_index]
        owner_prompt = prompt_of[slice_index, 0]
        prefix_state = lax.dynamic_index_in_dim(prompt_state, owner_prompt, 0, keepdims=False)
        tail = lax.dynamic_index_in_dim(prompt_tail, owner_prompt, 0, keepdims=False)
        token_weight = jnp.where(positions < live, adv_rows.astype(jnp.float32) / 1024.0, 0.0)
        extended = jnp.concatenate([tail, x_rows], axis=0).astype(jnp.float32)

        def scorer(ext_arg, state_arg):
            return local_scores(ext_arg, state_arg, b_rows, c_rows, dt_rows, upstream, token_weight, a_log, dt_bias, skip_gain, conv_w, conv_b)
        token_scores, pullback = jax.vjp(scorer, extended, prefix_state)
        grad_ext, grad_prefix = pullback(jnp.ones_like(token_scores))
        owner_mask = prompt_ids == owner_prompt
        acc_state = acc_state + jnp.where(owner_mask[:, None, None, None], grad_prefix[None], 0.0)
        acc_tail = acc_tail + jnp.where(owner_mask[:, None, None], grad_ext[:tail_len][None], 0.0)
        return ((acc_state, acc_tail), (token_scores, grad_ext[tail_len:].astype(jnp.bfloat16)))
    start_carry = (jnp.zeros(prompt_state.shape, jnp.float32), jnp.zeros((PROMPTS, tail_len, HEADS * HEAD_DIM), jnp.float32))
    (grad_state, grad_tail), (all_scores, all_grads) = lax.scan(step, start_carry, jnp.arange(DEVICES, dtype=jnp.int32))
    return (all_scores.reshape(TOKENS), all_grads.reshape(TOKENS, HEADS * HEAD_DIM), grad_state, grad_tail)
```

```python
import functools

import jax
import jax.numpy as jnp
from jax import lax
from jax.experimental import pallas as pl
from jax.experimental.pallas import tpu as pltpu
from jax.sharding import PartitionSpec as P

MESH = pl.DeviceIdType.MESH
F32 = jnp.float32
BF16 = jnp.bfloat16
LN2 = 0.6931471805599453
HIGHEST = lax.Precision.HIGHEST


def split(value):
    high = value.astype(BF16)
    return high, (value - high.astype(F32)).astype(BF16)


def dot(left, right):
    return lax.dot_general(left, right, (((1,), (0,)), ((), ())), preferred_element_type=F32)


def dot_t(left, right):
    return lax.dot_general(left, right, (((1,), (1,)), ((), ())), preferred_element_type=F32)


def gray(digit):
    return digit + digit // 2 - 2 * (digit // 2) * (digit % 2)


def kernel(
    planes,
    comps,
    x_hbm,
    dy_hbm,
    b_ref,
    c_ref,
    dtr_ref,
    adv_ref,
    len_ref,
    prompt_ref,
    alog_ref,
    dtb_ref,
    skip_ref,
    cw_ref,
    cb_ref,
    st_ref,
    tl_ref,
    score_ref,
    gx_hbm,
    gs_ref,
    gt_ref,
    xv,
    dyv,
    gxv,
    zh,
    zl,
    e1,
    e2,
    scale8,
    wcol,
    mth,
    mtl,
    ctv,
    kacc,
    pacc,
    sacc,
    xs,
    gsc,
    sall,
    tall,
    ssend,
    srecv,
    tsend,
    trecv,
    gsend,
    grecv,
    hsend,
    hrecv,
    zsend,
    zrecv,
    loc_sem,
    zs_sem,
    zt_sem,
    zg_sem,
    ss_sem,
    ts_sem,
    gsm_sem,
    hs_sem,
):
    toks = b_ref.shape[0]
    heads = alog_ref.shape[1]
    state = b_ref.shape[1]
    width = xv.shape[1] // comps
    z = lax.axis_index("prompt")
    me = lax.axis_index("comp")
    mx, my, mk = me // 8, (me // 2) % 4, me % 2

    def ahead(j):
        ox, oy, ok = gray(j // 8), gray((j // 2) % 4), j % 2
        return ((mx + ox) % 4 * 4 + (my + oy) % 4) * 2 + (mk + ok) % 2

    def behind(j):
        ox, oy, ok = gray(j // 8), gray((j // 2) % 4), j % 2
        return ((mx + 4 - ox) % 4 * 4 + (my + 4 - oy) % 4) * 2 + (mk + ok) % 2

    def plane_copy(src, dst, sems, j, target):
        return pltpu.make_async_remote_copy(
            src_ref=src,
            dst_ref=dst.at[me],
            send_sem=sems.at[0, j],
            recv_sem=sems.at[1, me],
            device_id=(z, target),
            device_id_type=MESH,
        )

    def plane_arrival(src, dst, sems, source):
        return pltpu.make_async_remote_copy(
            src_ref=src,
            dst_ref=dst.at[source],
            send_sem=sems.at[0, 0],
            recv_sem=sems.at[1, source],
            device_id=(z, source),
            device_id_type=MESH,
        )

    def line_copy(src, dst, sems, step):
        return pltpu.make_async_remote_copy(
            src_ref=src,
            dst_ref=dst.at[z],
            send_sem=sems.at[0, step],
            recv_sem=sems.at[1, z],
            device_id=((z + step) % planes, me),
            device_id_type=MESH,
        )

    def line_arrival(src, dst, sems, step):
        source = (z + planes - step) % planes
        return pltpu.make_async_remote_copy(
            src_ref=src,
            dst_ref=dst.at[source],
            send_sem=sems.at[0, step],
            recv_sem=sems.at[1, source],
            device_id=(source, me),
            device_id_type=MESH,
        )

    load_dy = pltpu.make_async_copy(dy_hbm, dyv, loc_sem.at[0])
    load_x = pltpu.make_async_copy(x_hbm, xv, loc_sem.at[1])
    load_dy.start()
    load_x.start()

    barrier = pltpu.get_barrier_semaphore()

    def greet(j, carry):
        pl.semaphore_signal(barrier, inc=1, device_id=(z, ahead(j)), device_id_type=MESH)
        return carry

    lax.fori_loop(1, comps, greet, 0)
    for step in range(1, planes):
        pl.semaphore_signal(
            barrier, inc=1, device_id=((z + step) % planes, me), device_id_type=MESH
        )

    sall[z] = st_ref[...].astype(BF16)
    xs[0:8, :] = jnp.zeros((8, width), F32)
    xs[5:8, :] = tl_ref[...].astype(F32)
    tall[z] = jnp.concatenate([xs[0:8, :], jnp.zeros((8, width), F32)], axis=0).astype(BF16)

    pl.semaphore_wait(barrier, comps - 1 + planes - 1)
    for step in range(1, planes):
        line_copy(tall.at[z], tall, zt_sem, step).start()
    for step in range(1, planes):
        line_copy(sall.at[z], sall, zs_sem, step).start()

    row = lax.broadcasted_iota(jnp.int32, (toks, toks), 0)
    col = lax.broadcasted_iota(jnp.int32, (toks, toks), 1)
    raw = dtr_ref[...] + dtb_ref[...]
    dt = jnp.maximum(raw, 0.0) + jnp.log1p(jnp.exp(-jnp.abs(raw)))
    total = lax.dot_general(
        jnp.where(row >= col, 1.0, 0.0),
        dt * jnp.exp(alog_ref[...]),
        (((1,), (0,)), ((), ())),
        precision=HIGHEST,
        preferred_element_type=F32,
    )
    power = jnp.floor(total[toks // 2 - 1 : toks // 2, :] * (1.0 / LN2) + 0.5)
    offset = total - power * LN2
    e1[...] = jnp.exp(-offset)
    e2[...] = dt * jnp.exp(offset)
    scale8[...] = jnp.broadcast_to(jnp.exp2(-power), (8, heads))
    weight = jnp.where(
        lax.broadcasted_iota(jnp.int32, (1, toks), 1) < len_ref[0],
        adv_ref[...].astype(F32) / 1024.0,
        0.0,
    )
    wcol[...] = jnp.broadcast_to(
        jnp.sum(jnp.where(row == col, weight, 0.0), axis=1, keepdims=True), (toks, 128)
    )
    high, low = split(jnp.where(row <= col, dot_t(b_ref[...], c_ref[...]), 0.0))
    mth[...] = high
    mtl[...] = low
    ctv[...] = jnp.transpose(c_ref[...].astype(F32)).astype(BF16)
    kacc[...] = jnp.zeros_like(kacc)
    pacc[...] = jnp.zeros_like(pacc)
    sacc[...] = jnp.zeros_like(sacc)
    gsc[0:8, :] = jnp.zeros((8, width), F32)
    gsc[8 + toks :, :] = jnp.zeros((8, width), F32)

    for step in range(1, planes):
        line_arrival(tall.at[z], tall, zt_sem, step).wait_recv()

    def send_tail(j, carry):
        target = ahead(j)
        tsend[j] = tall[prompt_ref[z * comps + target]]
        plane_copy(tsend.at[j], trecv, ts_sem, j, target).start()
        return carry

    lax.fori_loop(1, comps, send_tail, 0)
    trecv[me] = tall[prompt_ref[z * comps + me]]
    for step in range(1, planes):
        line_arrival(sall.at[z], sall, zs_sem, step).wait_recv()

    def send_state(j, carry):
        target = ahead(j)
        ssend[j] = sall[prompt_ref[z * comps + target]]
        plane_copy(ssend.at[j], srecv, ss_sem, j, target).start()
        return carry

    lax.fori_loop(1, comps, send_state, 0)
    srecv[me] = sall[prompt_ref[z * comps + me]]

    half = lax.broadcasted_iota(jnp.int32, (toks, 128), 1) // 64
    half8 = lax.broadcasted_iota(jnp.int32, (8, 128), 1) // 64
    group = width // 64

    def spread(value, index, block):
        parts = [
            jnp.take_along_axis(value, index + (block * group + 2 * i), axis=1)
            for i in range(width // 128)
        ]
        return jnp.concatenate(parts, axis=1)

    def lanes(value):
        return jnp.concatenate([value] * (width // 128), axis=1)

    load_dy.wait()

    def readout(j, carry):
        target = ahead(j)
        cols = pl.ds(pl.multiple_of(target * width, width), width)
        zval = spread(e1[...], half, target) * (lanes(wcol[...]) * dyv[:, cols].astype(F32))
        zhigh, zlow = split(zval)
        zh[target] = zhigh
        zl[target] = zlow
        part = dot(ctv[...], zhigh) + dot(ctv[...], zlow)
        part = part * spread(scale8[...], half8, target)[0:1, :]
        gsend[j] = part.astype(BF16)

        @pl.when(j > 0)
        def _():
            plane_copy(gsend.at[j], grecv, gsm_sem, j, target).start()

        return carry

    lax.fori_loop(0, comps, readout, 0)
    grecv[me] = gsend[0]

    load_x.wait()
    skip8 = jnp.broadcast_to(skip_ref[...], (8, heads))

    def mix(j, carry):
        block = behind(j)
        cols = pl.ds(pl.multiple_of(block * width, width), width)

        @pl.when(j > 0)
        def _():
            plane_arrival(tsend.at[0], trecv, ts_sem, block).wait_recv()

        xs[0:8, :] = trecv[block].astype(F32)[0:8, :]
        xs[8:, :] = xv[:, cols].astype(F32)
        taps = cw_ref[:, cols]
        conv = cb_ref[:, cols] + taps[3:4] * xs[8:, :]
        for k in range(3):
            conv = conv + taps[k : k + 1] * xs[5 + k : 5 + k + toks, :]
        sig = 0.5 * jnp.tanh(0.5 * conv) + 0.5
        act = conv * sig
        slope = sig + act * (1.0 - sig)
        late = spread(e2[...], half, block)
        vhigh, vlow = split(late * act)
        zhigh, zlow = zh[block], zl[block]
        kacc[...] += dot_t(zhigh, vhigh) + dot_t(zlow, vhigh) + dot_t(zhigh, vlow)
        back = dot(mth[...], zhigh) + dot(mth[...], zlow) + dot(mtl[...], zhigh)
        direct = spread(skip8, half8, block)[0:1, :] * (
            lanes(wcol[...]) * dyv[:, cols].astype(F32)
        )
        seen = act * direct
        sacc[...] += seen[:, :128] + seen[:, 128:]
        gsc[8 : 8 + toks, :] = (late * back + direct) * slope
        grad = taps[3:4] * gsc[0 : 8 + toks, :]
        for k in range(3):
            grad = grad + taps[k : k + 1] * gsc[3 - k : 11 - k + toks, :]
        gxv[:, cols] = grad[8:, :].astype(BF16)
        thigh = grad[0:8, :].astype(BF16).astype(F32)
        hsend[j] = jnp.concatenate([thigh, grad[0:8, :] - thigh], axis=0).astype(BF16)

        @pl.when(j > 0)
        def _():
            plane_copy(hsend.at[j], hrecv, hs_sem, j, block).start()

        return carry

    lax.fori_loop(0, comps, mix, 0)
    hrecv[me] = hsend[0]
    store_gx = pltpu.make_async_copy(gxv, gx_hbm, loc_sem.at[2])
    store_gx.start()

    def prefix(j, carry):
        block = behind(j)

        @pl.when(j > 0)
        def _():
            plane_arrival(ssend.at[0], srecv, ss_sem, block).wait_recv()

        scale = spread(scale8[...], half8, block)[0:1, :]
        scale = jnp.broadcast_to(scale, (toks, width)).astype(BF16)
        states = srecv[block]
        pacc[...] += dot(zh[block] * scale, states) + dot(zl[block] * scale, states)
        return carry

    lax.fori_loop(0, comps, prefix, 0)
    aff = dot_t(c_ref[...], b_ref[...])
    scores = (
        jnp.sum(jnp.where(row >= col, aff * kacc[...], 0.0), axis=1, keepdims=True)
        + jnp.sum(sacc[...], axis=1, keepdims=True)
        + jnp.sum(pacc[...] * c_ref[...].astype(F32), axis=1, keepdims=True)
    )
    score_ref[...] = jnp.sum(jnp.where(row == col, scores, 0.0), axis=0, keepdims=True)

    def arrive(j, carry):
        source = behind(j)
        plane_arrival(gsend.at[0], grecv, gsm_sem, source).wait_recv()
        plane_arrival(hsend.at[0], hrecv, hs_sem, source).wait_recv()
        return carry

    lax.fori_loop(1, comps, arrive, 0)

    def gather(r, carry):
        rows = pl.ds(pl.multiple_of(r * 16, 16), 16)
        sums = [jnp.zeros((16, width), F32) for _ in range(planes)]
        for source in range(comps):
            held = prompt_ref[z * comps + source]
            term = grecv[source, rows, :].astype(F32)
            sums = [sums[q] + jnp.where(held == q, term, 0.0) for q in range(planes)]
        for q in range(planes):
            zsend[q, rows, :] = sums[q]
        return carry

    lax.fori_loop(0, state // 16, gather, 0)
    sums = [jnp.zeros((8, width), F32) for _ in range(planes)]
    for source in range(comps):
        held = prompt_ref[z * comps + source]
        term = hrecv[source].astype(F32)
        term = term[0:8, :] + term[8:16, :]
        sums = [sums[q] + jnp.where(held == q, term, 0.0) for q in range(planes)]
    for q in range(planes):
        zsend[q, state:, :] = sums[q]
    for step in range(1, planes):
        line_copy(zsend.at[(z + step) % planes], zrecv, zg_sem, step).start()
    zrecv[z] = zsend[z]

    def leave(j, carry):
        plane_copy(tsend.at[j], trecv, ts_sem, j, ahead(j)).wait_send()
        plane_copy(ssend.at[j], srecv, ss_sem, j, ahead(j)).wait_send()
        plane_copy(gsend.at[j], grecv, gsm_sem, j, ahead(j)).wait_send()
        plane_copy(hsend.at[j], hrecv, hs_sem, j, behind(j)).wait_send()
        return carry

    lax.fori_loop(1, comps, leave, 0)
    for step in range(1, planes):
        line_copy(tall.at[z], tall, zt_sem, step).wait_send()
        line_copy(sall.at[z], sall, zs_sem, step).wait_send()
    for step in range(1, planes):
        line_arrival(zsend.at[0], zrecv, zg_sem, step).wait_recv()
    whole = zrecv[0] + zrecv[1]
    for q in range(2, planes):
        whole = whole + zrecv[q]
    gs_ref[...] = jnp.transpose(whole[0:state, :])
    gt_ref[...] = whole[state + 5 : state + 8, :]
    for step in range(1, planes):
        line_copy(zsend.at[(z + step) % planes], zrecv, zg_sem, step).wait_send()
    store_gx.wait()


def body(planes, comps):
    def run(
        x_in,
        b_in,
        c_in,
        dt_raw,
        dy_up,
        advantages,
        lengths,
        prompt_of,
        a_log,
        dt_bias,
        skip_gain,
        conv_w,
        conv_b,
        prompt_state,
        prompt_tail,
    ):
        toks, feats = x_in.shape
        heads = a_log.shape[0]
        state = b_in.shape[1]
        share = feats // comps
        tail_len = prompt_tail.shape[1]
        vmem = pl.BlockSpec(memory_space=pltpu.VMEM)
        smem = pl.BlockSpec(memory_space=pltpu.SMEM)
        hbm = pl.BlockSpec(memory_space=pl.ANY)
        pair = pltpu.SemaphoreType.DMA((2, comps))
        line = pltpu.SemaphoreType.DMA((2, planes))
        scores, grad_x, grad_state, grad_tail = pl.pallas_call(
            functools.partial(kernel, planes, comps),
            out_shape=(
                jax.ShapeDtypeStruct((1, toks), F32),
                jax.ShapeDtypeStruct((toks, feats), BF16),
                jax.ShapeDtypeStruct((share, state), F32),
                jax.ShapeDtypeStruct((tail_len, share), F32),
            ),
            in_specs=[hbm, hbm, vmem, vmem, vmem, vmem, smem, smem] + [vmem] * 7,
            out_specs=(vmem, hbm, vmem, vmem),
            scratch_shapes=[
                pltpu.VMEM((toks, feats), BF16),
                pltpu.VMEM((toks, feats), BF16),
                pltpu.VMEM((toks, feats), BF16),
                pltpu.VMEM((comps, toks, share), BF16),
                pltpu.VMEM((comps, toks, share), BF16),
                pltpu.VMEM((toks, heads), F32),
                pltpu.VMEM((toks, heads), F32),
                pltpu.VMEM((8, heads), F32),
                pltpu.VMEM((toks, 128), F32),
                pltpu.VMEM((toks, toks), BF16),
                pltpu.VMEM((toks, toks), BF16),
                pltpu.VMEM((state, toks), BF16),
                pltpu.VMEM((toks, toks), F32),
                pltpu.VMEM((toks, state), F32),
                pltpu.VMEM((toks, 128), F32),
                pltpu.VMEM((toks + 8, share), F32),
                pltpu.VMEM((toks + 16, share), F32),
                pltpu.VMEM((planes, share, state), BF16),
                pltpu.VMEM((planes, 16, share), BF16),
                pltpu.VMEM((comps, share, state), BF16),
                pltpu.VMEM((comps, share, state), BF16),
                pltpu.VMEM((comps, 16, share), BF16),
                pltpu.VMEM((comps, 16, share), BF16),
                pltpu.VMEM((comps, state, share), BF16),
                pltpu.VMEM((comps, state, share), BF16),
                pltpu.VMEM((comps, 16, share), BF16),
                pltpu.VMEM((comps, 16, share), BF16),
                pltpu.VMEM((planes, state + 8, share), F32),
                pltpu.VMEM((planes, state + 8, share), F32),
                pltpu.SemaphoreType.DMA((3,)),
                line,
                line,
                line,
                pair,
                pair,
                pair,
                pair,
            ],
            compiler_params=pltpu.CompilerParams(
                collective_id=0, has_side_effects=True, vmem_limit_bytes=56 << 20
            ),
            cost_estimate=pl.CostEstimate(
                flops=10 * toks * toks * feats,
                bytes_accessed=8 * toks * feats,
                transcendentals=toks * feats,
            ),
            name="mixer",
        )(
            x_in,
            dy_up,
            b_in,
            c_in,
            dt_raw,
            advantages.reshape(1, toks),
            lengths,
            prompt_of.reshape(-1),
            a_log.reshape(1, heads),
            dt_bias.reshape(1, heads),
            skip_gain.reshape(1, heads),
            conv_w,
            conv_b.reshape(1, feats),
            prompt_state.reshape(share, state),
            prompt_tail.reshape(tail_len, share),
        )
        return (
            scores.reshape(toks),
            grad_x,
            grad_state.reshape(prompt_state.shape),
            grad_tail.reshape(prompt_tail.shape),
        )

    return run


def solution(mesh):
    planes, comps = mesh.shape["prompt"], mesh.shape["comp"]
    both = P(("prompt", "comp"))
    rows = P(("prompt", "comp"), None)
    state = P("prompt", "comp", None, None)
    tail = P("prompt", None, "comp")
    in_specs = (rows,) * 5 + (both,) * 2 + (P(),) * 6 + (state, tail)
    out_specs = (both, rows, state, tail)
    return jax.shard_map(
        body(planes, comps), mesh=mesh, in_specs=in_specs, out_specs=out_specs, check_vma=False
    )
```

```python
import functools

import jax
import jax.numpy as jnp
from jax import lax
from jax.experimental import pallas as pl
from jax.experimental.pallas import tpu as pltpu
from jax.sharding import PartitionSpec as P

MESH = pl.DeviceIdType.MESH
F32 = jnp.float32
BF16 = jnp.bfloat16
LN2 = 0.6931471805599453
HIGHEST = lax.Precision.HIGHEST


def split(value):
    high = value.astype(BF16)
    return high, (value - high.astype(F32)).astype(BF16)


def dot(left, right):
    return lax.dot_general(left, right, (((1,), (0,)), ((), ())), preferred_element_type=F32)


def dot_t(left, right):
    return lax.dot_general(left, right, (((1,), (1,)), ((), ())), preferred_element_type=F32)


def gray(digit):
    return digit + digit // 2 - 2 * (digit // 2) * (digit % 2)


def kernel(
    planes,
    comps,
    x_hbm,
    dy_hbm,
    b_ref,
    c_ref,
    dtr_ref,
    adv_ref,
    len_ref,
    prompt_ref,
    alog_ref,
    dtb_ref,
    skip_ref,
    cw_ref,
    cb_ref,
    st_ref,
    tl_ref,
    score_ref,
    gx_hbm,
    gs_ref,
    gt_ref,
    xv,
    dyv,
    gxv,
    zh,
    zl,
    e1,
    e2,
    scale8,
    wcol,
    mth,
    mtl,
    lead,
    first,
    kacc,
    pacc,
    sacc,
    xs,
    gsc,
    xe,
    ge,
    sall,
    tall,
    ssend,
    srecv,
    tsend,
    trecv,
    gsend,
    grecv,
    hsend,
    hrecv,
    zsend,
    zrecv,
    loc_sem,
    zs_sem,
    zt_sem,
    zg_sem,
    ss_sem,
    ts_sem,
    gsm_sem,
    hs_sem,
):
    toks = b_ref.shape[0]
    heads = alog_ref.shape[1]
    state = b_ref.shape[1]
    width = xv.shape[1] // comps
    z = lax.axis_index("prompt")
    me = lax.axis_index("comp")
    mx, my, mk = me // 8, (me // 2) % 4, me % 2

    def ahead(j):
        ox, oy, ok = gray(j // 4 % 4), gray((j + j // 4) % 4), j // 16
        return ((mx + ox) % 4 * 4 + (my + oy) % 4) * 2 + (mk + ok) % 2

    def behind(j):
        ox, oy, ok = gray(j // 4 % 4), gray((j + j // 4) % 4), j // 16
        return ((mx + 4 - ox) % 4 * 4 + (my + 4 - oy) % 4) * 2 + (mk + ok) % 2

    def plane_copy(src, dst, sems, j, target):
        return pltpu.make_async_remote_copy(
            src_ref=src,
            dst_ref=dst.at[me],
            send_sem=sems.at[0, j],
            recv_sem=sems.at[1, me],
            device_id=(z, target),
            device_id_type=MESH,
        )

    def plane_arrival(src, dst, sems, source):
        return pltpu.make_async_remote_copy(
            src_ref=src,
            dst_ref=dst.at[source],
            send_sem=sems.at[0, 0],
            recv_sem=sems.at[1, source],
            device_id=(z, source),
            device_id_type=MESH,
        )

    def line_copy(src, dst, sems, step):
        return pltpu.make_async_remote_copy(
            src_ref=src,
            dst_ref=dst.at[z],
            send_sem=sems.at[0, step],
            recv_sem=sems.at[1, z],
            device_id=((z + step) % planes, me),
            device_id_type=MESH,
        )

    def line_arrival(src, dst, sems, step):
        source = (z + planes - step) % planes
        return pltpu.make_async_remote_copy(
            src_ref=src,
            dst_ref=dst.at[source],
            send_sem=sems.at[0, step],
            recv_sem=sems.at[1, source],
            device_id=(source, me),
            device_id_type=MESH,
        )

    load_dy = pltpu.make_async_copy(dy_hbm, dyv, loc_sem.at[0])
    load_x = pltpu.make_async_copy(x_hbm, xv, loc_sem.at[1])
    load_dy.start()
    load_x.start()

    barrier = pltpu.get_barrier_semaphore()

    def greet(j, carry):
        pl.semaphore_signal(barrier, inc=1, device_id=(z, ahead(j)), device_id_type=MESH)
        return carry

    lax.fori_loop(1, comps, greet, 0)
    for step in range(1, planes):
        pl.semaphore_signal(
            barrier, inc=1, device_id=((z + step) % planes, me), device_id_type=MESH
        )

    sall[z] = st_ref[...].astype(BF16)
    xe[0] = jnp.zeros((16, width), F32)
    xe[0, 5:8, :] = tl_ref[...].astype(F32)
    tall[z] = xe[0].astype(BF16)

    row = lax.broadcasted_iota(jnp.int32, (toks, toks), 0)
    col = lax.broadcasted_iota(jnp.int32, (toks, toks), 1)
    raw = dtr_ref[...] + dtb_ref[...]
    dt = jnp.maximum(raw, 0.0) + jnp.log1p(jnp.exp(-jnp.abs(raw)))
    total = lax.dot_general(
        jnp.where(row >= col, 1.0, 0.0),
        dt * jnp.exp(alog_ref[...]),
        (((1,), (0,)), ((), ())),
        precision=HIGHEST,
        preferred_element_type=F32,
    )
    power = jnp.floor(total[toks // 2 - 1 : toks // 2, :] * (1.0 / LN2) + 0.5)
    offset = total - power * LN2
    e1[...] = jnp.exp(-offset)
    e2[...] = dt * jnp.exp(offset)
    scale8[...] = jnp.broadcast_to(jnp.exp2(-power), (8, heads))
    weight = jnp.where(
        lax.broadcasted_iota(jnp.int32, (1, toks), 1) < len_ref[0],
        adv_ref[...].astype(F32) / 1024.0,
        0.0,
    )
    wcol[...] = jnp.broadcast_to(
        jnp.sum(jnp.where(row == col, weight, 0.0), axis=1, keepdims=True), (toks, 128)
    )
    high, low = split(jnp.where(row <= col, dot_t(b_ref[...], c_ref[...]), 0.0))
    mth[...] = high
    mtl[...] = low
    lead[0:state, :] = jnp.transpose(c_ref[...].astype(F32)).astype(BF16)
    lead[state : state + 16, :] = high[0:16, :]
    lead[state + 16 :, :] = low[0:16, :]
    kacc[...] = jnp.zeros_like(kacc)
    pacc[...] = jnp.zeros_like(pacc)
    sacc[...] = jnp.zeros_like(sacc)
    for u in range(2):
        gsc[u, toks:, :] = jnp.zeros((8, width), F32)

    pl.semaphore_wait(barrier, comps - 1 + planes - 1)
    for step in range(1, planes):
        line_copy(tall.at[z], tall, zt_sem, step).start()
    for step in range(1, planes):
        line_copy(sall.at[z], sall, zs_sem, step).start()

    half = lax.broadcasted_iota(jnp.int32, (toks, 128), 1) // 64
    half8 = lax.broadcasted_iota(jnp.int32, (8, 128), 1) // 64
    group = width // 64

    def spread(value, index, block):
        parts = [
            jnp.take_along_axis(value, index + (block * group + 2 * i), axis=1)
            for i in range(width // 128)
        ]
        return jnp.concatenate(parts, axis=1)

    def lanes(value):
        return jnp.concatenate([value] * (width // 128), axis=1)

    load_dy.wait()

    def readout(i, carry):
        for u in range(4):
            j = 4 * i + u
            target = ahead(j)
            cols = pl.ds(pl.multiple_of(target * width, width), width)
            zval = spread(e1[...], half, target) * (lanes(wcol[...]) * dyv[:, cols].astype(F32))
            zhigh, zlow = split(zval)
            zh[target] = zhigh
            zl[target] = zlow
            part = dot(lead[...], zhigh) + dot(lead[...], zlow)
            scale = spread(scale8[...], half8, target)[0:1, :]
            gsend[j] = (part[0:state, :] * scale).astype(BF16)
            first[target] = part[state : state + 8, :] + part[state + 16 : state + 24, :]
        for u in range(4):
            j = 4 * i + u

            def send():
                plane_copy(gsend.at[j], grecv, gsm_sem, j, ahead(j)).start()

            if u:
                send()
            else:
                pl.when(i > 0)(send)
        return carry

    lax.fori_loop(0, 2, readout, 0)

    for step in range(1, planes):
        line_arrival(tall.at[z], tall, zt_sem, step).wait_recv()

    def send_tail(j, carry):
        target = ahead(j)
        tsend[j] = tall[prompt_ref[z * comps + target]]
        plane_copy(tsend.at[j], trecv, ts_sem, j, target).start()
        return carry

    lax.fori_loop(1, comps, send_tail, 0)
    trecv[me] = tall[prompt_ref[z * comps + me]]
    lax.fori_loop(2, comps // 4, readout, 0)
    grecv[me] = gsend[0]

    load_x.wait()
    skip8 = jnp.broadcast_to(skip_ref[...], (8, heads))

    def arrive_tail(j, carry):
        plane_arrival(tsend.at[0], trecv, ts_sem, behind(j)).wait_recv()
        return carry

    lax.fori_loop(1, comps, arrive_tail, 0)

    def gate(conv):
        rise = jnp.tanh(conv) + 1.0
        act = conv * rise
        return act, rise + act * (2.0 - rise)

    def edge(i, carry):
        for u in range(4):
            j = 4 * i + u
            block = ahead(j)
            cols = pl.ds(pl.multiple_of(block * width, width), width)
            xe[u, 0:8, :] = trecv[block].astype(F32)[0:8, :]
            xe[u, 8:16, :] = xv[0:16, cols].astype(F32)[0:8, :]
            taps = 0.5 * cw_ref[:, cols]
            conv = 0.5 * cb_ref[:, cols] + taps[3:4] * xe[u, 8:16, :]
            for k in range(3):
                conv = conv + taps[k : k + 1] * xe[u, 5 + k : 13 + k, :]
            slope = gate(conv)[1]
            direct = spread(skip8, half8, block) * (
                lanes(wcol[0:8, :]) * dyv[0:16, cols].astype(F32)[0:8, :]
            )
            ge[u, 0:8, :] = jnp.zeros((8, width), F32)
            ge[u, 8:16, :] = (spread(e2[0:8, :], half8, block) * first[block] + direct) * slope
            grad = taps[3:4] * ge[u, 0:8, :]
            for k in range(3):
                grad = grad + taps[k : k + 1] * ge[u, 3 - k : 11 - k, :]
            high = grad.astype(BF16).astype(F32)
            hsend[j] = jnp.concatenate([high, grad - high], axis=0).astype(BF16)
        for u in range(4):
            j = 4 * i + u

            def send():
                plane_copy(hsend.at[j], hrecv, hs_sem, j, ahead(j)).start()

            if u:
                send()
            else:
                pl.when(i > 0)(send)
        return carry

    lax.fori_loop(0, comps // 4, edge, 0)
    hrecv[me] = hsend[0]

    for step in range(1, planes):
        line_arrival(sall.at[z], sall, zs_sem, step).wait_recv()

    def send_state(j, carry):
        target = ahead(j)
        ssend[j] = sall[prompt_ref[z * comps + target]]
        plane_copy(ssend.at[j], srecv, ss_sem, j, target).start()
        return carry

    lax.fori_loop(1, comps, send_state, 0)
    srecv[me] = sall[prompt_ref[z * comps + me]]

    def mix(i, carry):
        for u in range(2):
            block = 2 * i + u
            cols = pl.ds(pl.multiple_of(block * width, width), width)
            xs[u, 0:8, :] = trecv[block].astype(F32)[0:8, :]
            xs[u, 8:, :] = xv[:, cols].astype(F32)
            taps = 0.5 * cw_ref[:, cols]
            conv = 0.5 * cb_ref[:, cols] + taps[3:4] * xs[u, 8:, :]
            for k in range(3):
                conv = conv + taps[k : k + 1] * xs[u, 5 + k : 5 + k + toks, :]
            act, slope = gate(conv)
            late = spread(e2[...], half, block)
            vhigh, vlow = split(late * act)
            zhigh, zlow = zh[block], zl[block]
            kacc[...] += dot_t(zhigh, vhigh) + dot_t(zlow, vhigh) + dot_t(zhigh, vlow)
            back = dot(mth[...], zhigh) + dot(mth[...], zlow) + dot(mtl[...], zhigh)
            direct = spread(skip8, half8, block)[0:1, :] * (
                lanes(wcol[...]) * dyv[:, cols].astype(F32)
            )
            seen = act * direct
            sacc[...] += seen[:, :128] + seen[:, 128:]
            gsc[u, 0:toks, :] = (late * back + direct) * slope
            grad = taps[3:4] * gsc[u, 0:toks, :]
            for k in range(3):
                grad = grad + taps[k : k + 1] * gsc[u, 3 - k : 3 - k + toks, :]
            gxv[:, cols] = grad.astype(BF16)
        return carry

    lax.fori_loop(0, comps // 2, mix, 0)
    store_gx = pltpu.make_async_copy(gxv, gx_hbm, loc_sem.at[2])
    store_gx.start()

    def arrive(j, carry):
        source = behind(j)
        plane_arrival(gsend.at[0], grecv, gsm_sem, source).wait_recv()
        plane_arrival(hsend.at[0], hrecv, hs_sem, source).wait_recv()
        return carry

    lax.fori_loop(1, comps, arrive, 0)

    def gather(r, carry):
        rows = pl.ds(pl.multiple_of(r * 16, 16), 16)
        sums = [jnp.zeros((16, width), F32) for _ in range(planes)]
        for source in range(comps):
            held = prompt_ref[z * comps + source]
            term = grecv[source, rows, :].astype(F32)
            sums = [sums[q] + jnp.where(held == q, term, 0.0) for q in range(planes)]
        for q in range(planes):
            zsend[q, rows, :] = sums[q]
        return carry

    lax.fori_loop(0, state // 16, gather, 0)
    sums = [jnp.zeros((8, width), F32) for _ in range(planes)]
    for source in range(comps):
        held = prompt_ref[z * comps + source]
        term = hrecv[source].astype(F32)
        term = term[0:8, :] + term[8:16, :]
        sums = [sums[q] + jnp.where(held == q, term, 0.0) for q in range(planes)]
    for q in range(planes):
        zsend[q, state:, :] = sums[q]
    for step in range(1, planes):
        line_copy(zsend.at[(z + step) % planes], zrecv, zg_sem, step).start()
    zrecv[z] = zsend[z]

    def prefix(i, carry):
        for u in range(4):
            j = 4 * i + u

            def arrive_state():
                plane_arrival(ssend.at[0], srecv, ss_sem, behind(j)).wait_recv()

            if u:
                arrive_state()
            else:
                pl.when(i > 0)(arrive_state)
        total = pacc[...]
        for u in range(4):
            block = behind(4 * i + u)
            scales = [
                jnp.take_along_axis(
                    scale8[...], jnp.full((8, 128), block * group + g, jnp.int32), axis=1
                )[0:1, :]
                for g in range(group)
            ]
            states = jnp.concatenate(
                [
                    srecv[block, 64 * g : 64 * g + 64, :].astype(F32) * scales[g]
                    for g in range(group)
                ],
                axis=0,
            ).astype(BF16)
            total = total + dot(zh[block], states) + dot(zl[block], states)
        pacc[...] = total
        return carry

    lax.fori_loop(0, comps // 4, prefix, 0)
    aff = dot_t(c_ref[...], b_ref[...])
    scores = (
        jnp.sum(jnp.where(row >= col, aff * kacc[...], 0.0), axis=1, keepdims=True)
        + jnp.sum(sacc[...], axis=1, keepdims=True)
        + jnp.sum(pacc[...] * c_ref[...].astype(F32), axis=1, keepdims=True)
    )
    score_ref[...] = jnp.sum(jnp.where(row == col, scores, 0.0), axis=0, keepdims=True)

    def leave(j, carry):
        plane_copy(tsend.at[j], trecv, ts_sem, j, ahead(j)).wait_send()
        plane_copy(ssend.at[j], srecv, ss_sem, j, ahead(j)).wait_send()
        plane_copy(gsend.at[j], grecv, gsm_sem, j, ahead(j)).wait_send()
        plane_copy(hsend.at[j], hrecv, hs_sem, j, ahead(j)).wait_send()
        return carry

    lax.fori_loop(1, comps, leave, 0)
    for step in range(1, planes):
        line_copy(tall.at[z], tall, zt_sem, step).wait_send()
        line_copy(sall.at[z], sall, zs_sem, step).wait_send()
    for step in range(1, planes):
        line_arrival(zsend.at[0], zrecv, zg_sem, step).wait_recv()
    whole = zrecv[0] + zrecv[1]
    for q in range(2, planes):
        whole = whole + zrecv[q]
    gs_ref[...] = jnp.transpose(whole[0:state, :])
    gt_ref[...] = whole[state:, :]
    for step in range(1, planes):
        line_copy(zsend.at[(z + step) % planes], zrecv, zg_sem, step).wait_send()
    store_gx.wait()


def finish(gx_in, score_in, gs_in, gt_in, score_ref, gx_ref, gs_ref, gt_ref, sem):
    copy = pltpu.make_async_copy(gx_in, gx_ref, sem)
    copy.start()
    score_ref[...] = score_in[...]
    gs_ref[...] = gs_in[...]
    gt_ref[...] = gt_in[5:8, :].reshape(gt_ref.shape)
    copy.wait()


def body(planes, comps):
    def run(
        x_in,
        b_in,
        c_in,
        dt_raw,
        dy_up,
        advantages,
        lengths,
        prompt_of,
        a_log,
        dt_bias,
        skip_gain,
        conv_w,
        conv_b,
        prompt_state,
        prompt_tail,
    ):
        toks, feats = x_in.shape
        heads = a_log.shape[0]
        state = b_in.shape[1]
        share = feats // comps
        tail_len = prompt_tail.shape[1]
        vmem = pl.BlockSpec(memory_space=pltpu.VMEM)
        smem = pl.BlockSpec(memory_space=pltpu.SMEM)
        off = pl.BlockSpec(memory_space=pltpu.HBM)
        hbm = pl.BlockSpec(memory_space=pl.ANY)
        pair = pltpu.SemaphoreType.DMA((2, comps))
        line = pltpu.SemaphoreType.DMA((2, planes))
        scores, grad_x, grad_state, grad_tail = pl.pallas_call(
            functools.partial(kernel, planes, comps),
            out_shape=(
                jax.ShapeDtypeStruct((1, toks), F32),
                jax.ShapeDtypeStruct((toks, feats), BF16),
                jax.ShapeDtypeStruct((share, state), F32),
                jax.ShapeDtypeStruct((8, share), F32),
            ),
            in_specs=[off, off, vmem, vmem, vmem, vmem, smem, smem] + [vmem] * 7,
            out_specs=(vmem, hbm, vmem, vmem),
            scratch_shapes=[
                pltpu.VMEM((toks, feats), BF16),
                pltpu.VMEM((toks, feats), BF16),
                pltpu.VMEM((toks, feats), BF16),
                pltpu.VMEM((comps, toks, share), BF16),
                pltpu.VMEM((comps, toks, share), BF16),
                pltpu.VMEM((toks, heads), F32),
                pltpu.VMEM((toks, heads), F32),
                pltpu.VMEM((8, heads), F32),
                pltpu.VMEM((toks, 128), F32),
                pltpu.VMEM((toks, toks), BF16),
                pltpu.VMEM((toks, toks), BF16),
                pltpu.VMEM((state + 32, toks), BF16),
                pltpu.VMEM((comps, 8, share), F32),
                pltpu.VMEM((toks, toks), F32),
                pltpu.VMEM((toks, state), F32),
                pltpu.VMEM((toks, 128), F32),
                pltpu.VMEM((2, toks + 8, share), F32),
                pltpu.VMEM((2, toks + 8, share), F32),
                pltpu.VMEM((4, 16, share), F32),
                pltpu.VMEM((4, 16, share), F32),
                pltpu.VMEM((planes, share, state), BF16),
                pltpu.VMEM((planes, 16, share), BF16),
                pltpu.VMEM((comps, share, state), BF16),
                pltpu.VMEM((comps, share, state), BF16),
                pltpu.VMEM((comps, 16, share), BF16),
                pltpu.VMEM((comps, 16, share), BF16),
                pltpu.VMEM((comps, state, share), BF16),
                pltpu.VMEM((comps, state, share), BF16),
                pltpu.VMEM((comps, 16, share), BF16),
                pltpu.VMEM((comps, 16, share), BF16),
                pltpu.VMEM((planes, state + 8, share), F32),
                pltpu.VMEM((planes, state + 8, share), F32),
                pltpu.SemaphoreType.DMA((3,)),
                line,
                line,
                line,
                pair,
                pair,
                pair,
                pair,
            ],
            compiler_params=pltpu.CompilerParams(
                collective_id=0, has_side_effects=True, vmem_limit_bytes=56 << 20
            ),
            cost_estimate=pl.CostEstimate(
                flops=10 * toks * toks * feats,
                bytes_accessed=8 * toks * feats,
                transcendentals=toks * feats,
            ),
            name="mixer",
        )(
            x_in,
            dy_up,
            b_in,
            c_in,
            dt_raw,
            advantages.reshape(1, toks),
            lengths,
            prompt_of.reshape(-1),
            a_log.reshape(1, heads),
            dt_bias.reshape(1, heads),
            skip_gain.reshape(1, heads),
            conv_w,
            conv_b.reshape(1, feats),
            prompt_state.reshape(share, state),
            prompt_tail.reshape(tail_len, share),
        )
        scores, grad_x, grad_state, grad_tail = pl.pallas_call(
            finish,
            out_shape=(
                jax.ShapeDtypeStruct((1, toks), F32),
                jax.ShapeDtypeStruct((toks, feats), BF16),
                jax.ShapeDtypeStruct((share, state), F32),
                jax.ShapeDtypeStruct((tail_len, 1, share), F32),
            ),
            in_specs=[off, vmem, vmem, vmem],
            out_specs=(vmem, off, vmem, vmem),
            scratch_shapes=[pltpu.SemaphoreType.DMA],
            compiler_params=pltpu.CompilerParams(vmem_limit_bytes=4 << 20),
            name="finish",
        )(grad_x, scores, grad_state, grad_tail)
        return (
            scores.reshape(toks),
            grad_x,
            grad_state.reshape(prompt_state.shape),
            grad_tail.reshape(tail_len, 1, share).transpose(1, 0, 2),
        )

    return run


def solution(mesh):
    planes, comps = mesh.shape["prompt"], mesh.shape["comp"]
    both = P(("prompt", "comp"))
    rows = P(("prompt", "comp"), None)
    state = P("prompt", "comp", None, None)
    tail = P("prompt", None, "comp")
    in_specs = (rows,) * 5 + (both,) * 2 + (P(),) * 6 + (state, tail)
    out_specs = (both, rows, state, tail)
    return jax.shard_map(
        body(planes, comps), mesh=mesh, in_specs=in_specs, out_specs=out_specs, check_vma=False
    )
```

```python
import functools

import jax
import jax.numpy as jnp
from jax import lax
from jax.experimental import pallas as pl
from jax.experimental.pallas import tpu as pltpu
from jax.sharding import PartitionSpec as P

MESH = pl.DeviceIdType.MESH
F32 = jnp.float32
BF16 = jnp.bfloat16
LN2 = 0.6931471805599453
HIGHEST = lax.Precision.HIGHEST


def split(value):
    high = value.astype(BF16)
    return high, (value - high.astype(F32)).astype(BF16)


def dot(left, right):
    return lax.dot_general(left, right, (((1,), (0,)), ((), ())), preferred_element_type=F32)


def dot_t(left, right):
    return lax.dot_general(left, right, (((1,), (1,)), ((), ())), preferred_element_type=F32)


def offsets(j):
    row = lax.rem(lax.div(j, 4), 4)
    return lax.rem(j, 4), lax.rem(j + row, 4), lax.div(j, 16)


def kernel(
    planes,
    comps,
    x_hbm,
    dy_hbm,
    b_ref,
    c_ref,
    dtr_ref,
    adv_ref,
    len_ref,
    prompt_ref,
    alog_ref,
    dtb_ref,
    skip_ref,
    cw_ref,
    cb_ref,
    st_ref,
    tl_ref,
    score_ref,
    gx_hbm,
    gs_ref,
    gt_ref,
    xv,
    dyv,
    gxv,
    zh,
    zl,
    e1,
    e2,
    scale8,
    wcol,
    mth,
    mtl,
    lead,
    first,
    kacc,
    pacc,
    sacc,
    xs,
    gsc,
    xe,
    ge,
    sall,
    tall,
    ssend,
    srecv,
    tsend,
    trecv,
    gsend,
    grecv,
    hsend,
    hrecv,
    zsend,
    zrecv,
    loc_sem,
    zs_sem,
    zt_sem,
    zg_sem,
    ss_sem,
    ts_sem,
    gsm_sem,
    hs_sem,
):
    toks = b_ref.shape[0]
    heads = alog_ref.shape[1]
    state = b_ref.shape[1]
    width = xv.shape[1] // comps
    z = lax.axis_index("prompt")
    me = lax.axis_index("comp")
    mx, my, mk = lax.div(me, 8), lax.rem(lax.div(me, 2), 4), lax.rem(me, 2)

    def ahead(j):
        ox, oy, ok = offsets(jnp.int32(j))
        return (lax.rem(mx + ox, 4) * 4 + lax.rem(my + oy, 4)) * 2 + lax.rem(mk + ok, 2)

    def behind(j):
        ox, oy, ok = offsets(jnp.int32(j))
        return (lax.rem(mx + 4 - ox, 4) * 4 + lax.rem(my + 4 - oy, 4)) * 2 + lax.rem(mk + ok, 2)

    def plane_copy(src, dst, sems, j, target):
        return pltpu.make_async_remote_copy(
            src_ref=src,
            dst_ref=dst.at[me],
            send_sem=sems.at[0, j],
            recv_sem=sems.at[1, me],
            device_id=(z, target),
            device_id_type=MESH,
        )

    def plane_arrival(src, dst, sems, source):
        return pltpu.make_async_remote_copy(
            src_ref=src,
            dst_ref=dst.at[source],
            send_sem=sems.at[0, 0],
            recv_sem=sems.at[1, source],
            device_id=(z, source),
            device_id_type=MESH,
        )

    def line_copy(src, dst, sems, step):
        return pltpu.make_async_remote_copy(
            src_ref=src,
            dst_ref=dst.at[z],
            send_sem=sems.at[0, step],
            recv_sem=sems.at[1, z],
            device_id=((z + step) % planes, me),
            device_id_type=MESH,
        )

    def line_arrival(src, dst, sems, step):
        source = (z + planes - step) % planes
        return pltpu.make_async_remote_copy(
            src_ref=src,
            dst_ref=dst.at[source],
            send_sem=sems.at[0, step],
            recv_sem=sems.at[1, source],
            device_id=(source, me),
            device_id_type=MESH,
        )

    load_dy = pltpu.make_async_copy(dy_hbm, dyv, loc_sem.at[0])
    load_x = pltpu.make_async_copy(x_hbm, xv, loc_sem.at[1])
    load_dy.start()
    load_x.start()

    barrier = pltpu.get_barrier_semaphore()

    def greet(j, carry):
        pl.semaphore_signal(barrier, inc=1, device_id=(z, ahead(j)), device_id_type=MESH)
        return carry

    lax.fori_loop(1, comps, greet, 0)
    for step in range(1, planes):
        pl.semaphore_signal(
            barrier, inc=1, device_id=((z + step) % planes, me), device_id_type=MESH
        )

    sall[z] = st_ref[...].astype(BF16)
    xe[0] = jnp.zeros((16, width), F32)
    xe[0, 5:8, :] = tl_ref[...].astype(F32)
    tall[z] = xe[0].astype(BF16)

    row = lax.broadcasted_iota(jnp.int32, (toks, toks), 0)
    col = lax.broadcasted_iota(jnp.int32, (toks, toks), 1)
    raw = dtr_ref[...] + dtb_ref[...]
    dt = jnp.maximum(raw, 0.0) + jnp.log1p(jnp.exp(-jnp.abs(raw)))
    total = lax.dot_general(
        jnp.where(row >= col, 1.0, 0.0),
        dt * jnp.exp(alog_ref[...]),
        (((1,), (0,)), ((), ())),
        precision=HIGHEST,
        preferred_element_type=F32,
    )
    power = jnp.floor(total[toks // 2 - 1 : toks // 2, :] * (1.0 / LN2) + 0.5)
    offset = total - power * LN2
    e1[...] = jnp.exp(-offset)
    e2[...] = dt * jnp.exp(offset)
    scale8[...] = jnp.broadcast_to(jnp.exp2(-power), (8, heads))
    weight = jnp.where(
        lax.broadcasted_iota(jnp.int32, (1, toks), 1) < len_ref[0],
        adv_ref[...].astype(F32) / 1024.0,
        0.0,
    )
    wcol[...] = jnp.broadcast_to(
        jnp.sum(jnp.where(row == col, weight, 0.0), axis=1, keepdims=True), (toks, 128)
    )
    high, low = split(jnp.where(row <= col, dot_t(b_ref[...], c_ref[...]), 0.0))
    mth[...] = high
    mtl[...] = low
    lead[0:state, :] = jnp.transpose(c_ref[...].astype(F32)).astype(BF16)
    lead[state : state + 16, :] = high[0:16, :]
    lead[state + 16 :, :] = low[0:16, :]
    kacc[...] = jnp.zeros_like(kacc)
    pacc[...] = jnp.zeros_like(pacc)
    sacc[...] = jnp.zeros_like(sacc)
    for u in range(2):
        gsc[u, toks:, :] = jnp.zeros((8, width), F32)

    pl.semaphore_wait(barrier, comps - 1 + planes - 1)
    for step in range(1, planes):
        line_copy(tall.at[z], tall, zt_sem, step).start()
    for step in range(1, planes):
        line_copy(sall.at[z], sall, zs_sem, step).start()

    half = lax.broadcasted_iota(jnp.int32, (toks, 128), 1) // 64
    half8 = lax.broadcasted_iota(jnp.int32, (8, 128), 1) // 64
    group = width // 64

    def spread(value, index, block):
        parts = [
            jnp.take_along_axis(value, index + (block * group + 2 * i), axis=1)
            for i in range(width // 128)
        ]
        return jnp.concatenate(parts, axis=1)

    def lanes(value):
        return jnp.concatenate([value] * (width // 128), axis=1)

    load_dy.wait()

    def readout(i, carry):
        for u in range(4):
            j = 4 * i + u
            target = ahead(j)
            cols = pl.ds(pl.multiple_of(target * width, width), width)
            zval = spread(e1[...], half, target) * (lanes(wcol[...]) * dyv[:, cols].astype(F32))
            zhigh, zlow = split(zval)
            zh[target] = zhigh
            zl[target] = zlow
            part = dot(lead[...], zhigh) + dot(lead[...], zlow)
            scale = spread(scale8[...], half8, target)[0:1, :]
            gsend[j] = (part[0:state, :] * scale).astype(BF16)
            first[target] = part[state : state + 8, :] + part[state + 16 : state + 24, :]
        for u in range(4):
            j = 4 * i + u

            def send():
                plane_copy(gsend.at[j], grecv, gsm_sem, j, ahead(j)).start()

            if u:
                send()
            else:
                pl.when(i > 0)(send)
        return carry

    lax.fori_loop(0, 2, readout, 0)

    for step in range(1, planes):
        line_arrival(tall.at[z], tall, zt_sem, step).wait_recv()

    def send_tail(j, carry):
        target = ahead(j)
        tsend[j] = tall[prompt_ref[z * comps + target]]
        plane_copy(tsend.at[j], trecv, ts_sem, j, target).start()
        return carry

    lax.fori_loop(1, comps, send_tail, 0)
    trecv[me] = tall[prompt_ref[z * comps + me]]
    lax.fori_loop(2, comps // 4, readout, 0)
    grecv[me] = gsend[0]

    load_x.wait()
    skip8 = jnp.broadcast_to(skip_ref[...], (8, heads))

    def arrive_tail(j, carry):
        plane_arrival(tsend.at[0], trecv, ts_sem, lax.rem(me + j, comps)).wait_recv()
        return carry

    lax.fori_loop(1, comps, arrive_tail, 0)

    def gate(conv):
        rise = jnp.tanh(conv) + 1.0
        act = conv * rise
        return act, rise + act * (2.0 - rise)

    def edge(i, carry):
        for u in range(4):
            j = 4 * i + u
            block = ahead(j)
            cols = pl.ds(pl.multiple_of(block * width, width), width)
            xe[u, 0:8, :] = trecv[block].astype(F32)[0:8, :]
            xe[u, 8:16, :] = xv[0:16, cols].astype(F32)[0:8, :]
            taps = 0.5 * cw_ref[:, cols]
            conv = 0.5 * cb_ref[:, cols] + taps[3:4] * xe[u, 8:16, :]
            for k in range(3):
                conv = conv + taps[k : k + 1] * xe[u, 5 + k : 13 + k, :]
            slope = gate(conv)[1]
            direct = spread(skip8, half8, block) * (
                lanes(wcol[0:8, :]) * dyv[0:16, cols].astype(F32)[0:8, :]
            )
            ge[u, 0:8, :] = jnp.zeros((8, width), F32)
            ge[u, 8:16, :] = (spread(e2[0:8, :], half8, block) * first[block] + direct) * slope
            grad = taps[3:4] * ge[u, 0:8, :]
            for k in range(3):
                grad = grad + taps[k : k + 1] * ge[u, 3 - k : 11 - k, :]
            high = grad.astype(BF16).astype(F32)
            hsend[j] = jnp.concatenate([high, grad - high], axis=0).astype(BF16)
        for u in range(4):
            j = 4 * i + u

            def send():
                plane_copy(hsend.at[j], hrecv, hs_sem, j, ahead(j)).start()

            if u:
                send()
            else:
                pl.when(i > 0)(send)
        return carry

    lax.fori_loop(0, comps // 4, edge, 0)
    hrecv[me] = hsend[0]

    for step in range(1, planes):
        line_arrival(sall.at[z], sall, zs_sem, step).wait_recv()

    def send_state(j, carry):
        target = ahead(j)
        ssend[j] = sall[prompt_ref[z * comps + target]]
        plane_copy(ssend.at[j], srecv, ss_sem, j, target).start()
        return carry

    lax.fori_loop(1, comps, send_state, 0)
    srecv[me] = sall[prompt_ref[z * comps + me]]

    def mix(i, carry):
        for u in range(2):
            block = 2 * i + u
            cols = pl.ds(pl.multiple_of(block * width, width), width)
            xs[u, 0:8, :] = trecv[block].astype(F32)[0:8, :]
            xs[u, 8:, :] = xv[:, cols].astype(F32)
            taps = 0.5 * cw_ref[:, cols]
            conv = 0.5 * cb_ref[:, cols] + taps[3:4] * xs[u, 8:, :]
            for k in range(3):
                conv = conv + taps[k : k + 1] * xs[u, 5 + k : 5 + k + toks, :]
            act, slope = gate(conv)
            late = spread(e2[...], half, block)
            vhigh, vlow = split(late * act)
            zhigh, zlow = zh[block], zl[block]
            kacc[...] += dot_t(zhigh, vhigh) + dot_t(zlow, vhigh) + dot_t(zhigh, vlow)
            back = dot(mth[...], zhigh) + dot(mth[...], zlow) + dot(mtl[...], zhigh)
            direct = spread(skip8, half8, block)[0:1, :] * (
                lanes(wcol[...]) * dyv[:, cols].astype(F32)
            )
            seen = act * direct
            sacc[...] += seen[:, :128] + seen[:, 128:]
            gsc[u, 0:toks, :] = (late * back + direct) * slope
            grad = taps[3:4] * gsc[u, 0:toks, :]
            for k in range(3):
                grad = grad + taps[k : k + 1] * gsc[u, 3 - k : 3 - k + toks, :]
            gxv[:, cols] = grad.astype(BF16)
        return carry

    lax.fori_loop(0, comps // 2, mix, 0)
    store_gx = pltpu.make_async_copy(gxv, gx_hbm, loc_sem.at[2])
    store_gx.start()

    def arrive(j, carry):
        source = lax.rem(me + j, comps)
        plane_arrival(gsend.at[0], grecv, gsm_sem, source).wait_recv()
        plane_arrival(hsend.at[0], hrecv, hs_sem, source).wait_recv()
        return carry

    lax.fori_loop(1, comps, arrive, 0)

    def gather(r, carry):
        rows = pl.ds(pl.multiple_of(r * 16, 16), 16)
        sums = [jnp.zeros((16, width), F32) for _ in range(planes)]
        for source in range(comps):
            held = prompt_ref[z * comps + source]
            term = grecv[source, rows, :].astype(F32)
            sums = [sums[q] + jnp.where(held == q, term, 0.0) for q in range(planes)]
        for q in range(planes):
            zsend[q, rows, :] = sums[q]
        return carry

    lax.fori_loop(0, state // 16, gather, 0)
    sums = [jnp.zeros((8, width), F32) for _ in range(planes)]
    for source in range(comps):
        held = prompt_ref[z * comps + source]
        term = hrecv[source].astype(F32)
        term = term[0:8, :] + term[8:16, :]
        sums = [sums[q] + jnp.where(held == q, term, 0.0) for q in range(planes)]
    for q in range(planes):
        zsend[q, state:, :] = sums[q]
    for step in range(1, planes):
        line_copy(zsend.at[(z + step) % planes], zrecv, zg_sem, step).start()
    zrecv[z] = zsend[z]

    beside = lax.rem(me + 1, comps)

    def leave(j, carry):
        plane_copy(tsend.at[j], trecv, ts_sem, j, beside).wait_send()
        plane_copy(gsend.at[j], grecv, gsm_sem, j, beside).wait_send()
        plane_copy(hsend.at[j], hrecv, hs_sem, j, beside).wait_send()
        return carry

    lax.fori_loop(1, comps, leave, 0)

    def prefix(i, carry):
        for u in range(4):
            j = 4 * i + u

            def arrive_state():
                plane_arrival(ssend.at[0], srecv, ss_sem, behind(j)).wait_recv()

            if u:
                arrive_state()
            else:
                pl.when(i > 0)(arrive_state)
        total = pacc[...]
        for u in range(4):
            block = behind(4 * i + u)
            scales = [
                jnp.take_along_axis(
                    scale8[...], jnp.full((8, 128), block * group + g, jnp.int32), axis=1
                )[0:1, :]
                for g in range(group)
            ]
            states = jnp.concatenate(
                [
                    srecv[block, 64 * g : 64 * g + 64, :].astype(F32) * scales[g]
                    for g in range(group)
                ],
                axis=0,
            ).astype(BF16)
            total = total + dot(zh[block], states) + dot(zl[block], states)
        pacc[...] = total
        return carry

    lax.fori_loop(0, comps // 4, prefix, 0)
    aff = dot_t(c_ref[...], b_ref[...])
    scores = (
        jnp.sum(jnp.where(row >= col, aff * kacc[...], 0.0), axis=1, keepdims=True)
        + jnp.sum(sacc[...], axis=1, keepdims=True)
        + jnp.sum(pacc[...] * c_ref[...].astype(F32), axis=1, keepdims=True)
    )
    score_ref[...] = jnp.sum(jnp.where(row == col, scores, 0.0), axis=0, keepdims=True)

    def leave_state(j, carry):
        plane_copy(ssend.at[j], srecv, ss_sem, j, beside).wait_send()
        return carry

    lax.fori_loop(1, comps, leave_state, 0)
    for step in range(1, planes):
        line_copy(tall.at[z], tall, zt_sem, step).wait_send()
        line_copy(sall.at[z], sall, zs_sem, step).wait_send()
    for step in range(1, planes):
        line_arrival(zsend.at[0], zrecv, zg_sem, step).wait_recv()
    whole = zrecv[0] + zrecv[1]
    for q in range(2, planes):
        whole = whole + zrecv[q]
    gs_ref[...] = jnp.transpose(whole[0:state, :])
    gt_ref[...] = whole[state + 5 : state + 8, :].reshape(gt_ref.shape)
    for step in range(1, planes):
        line_copy(zsend.at[(z + step) % planes], zrecv, zg_sem, step).wait_send()
    store_gx.wait()


def finish(parts, *refs):
    sources, targets, held, sems = refs[0:4], refs[4:8], refs[8:12], refs[12]
    rows = held[1].shape[0] // parts
    spans = [(1, pl.ds(rows * i, rows)) for i in range(parts)] + [
        (i, pl.ds(0, held[i].shape[0])) for i in (0, 2, 3)
    ]
    loads = [
        pltpu.make_async_copy(sources[i].at[span], held[i].at[span], sems.at[0, n])
        for n, (i, span) in enumerate(spans)
    ]
    stores = [
        pltpu.make_async_copy(held[i].at[span], targets[i].at[span], sems.at[1, n])
        for n, (i, span) in enumerate(spans)
    ]
    for load in loads:
        load.start()
    for load, store in zip(loads, stores):
        load.wait()
        store.start()
    for store in stores:
        store.wait()


def body(planes, comps):
    def run(
        x_in,
        b_in,
        c_in,
        dt_raw,
        dy_up,
        advantages,
        lengths,
        prompt_of,
        a_log,
        dt_bias,
        skip_gain,
        conv_w,
        conv_b,
        prompt_state,
        prompt_tail,
    ):
        toks, feats = x_in.shape
        heads = a_log.shape[0]
        state = b_in.shape[1]
        share = feats // comps
        tail_len = prompt_tail.shape[1]
        vmem = pl.BlockSpec(memory_space=pltpu.VMEM)
        smem = pl.BlockSpec(memory_space=pltpu.SMEM)
        off = pl.BlockSpec(memory_space=pltpu.HBM)
        hbm = pl.BlockSpec(memory_space=pl.ANY)
        pair = pltpu.SemaphoreType.DMA((2, comps))
        line = pltpu.SemaphoreType.DMA((2, planes))
        scores, grad_x, grad_state, grad_tail = pl.pallas_call(
            functools.partial(kernel, planes, comps),
            out_shape=(
                jax.ShapeDtypeStruct((1, toks), F32),
                jax.ShapeDtypeStruct((toks, feats), BF16),
                jax.ShapeDtypeStruct((share, state), F32),
                jax.ShapeDtypeStruct((tail_len, 1, share), F32),
            ),
            in_specs=[off, off, vmem, vmem, vmem, vmem, smem, smem] + [vmem] * 7,
            out_specs=(vmem, hbm, vmem, vmem),
            scratch_shapes=[
                pltpu.VMEM((toks, feats), BF16),
                pltpu.VMEM((toks, feats), BF16),
                pltpu.VMEM((toks, feats), BF16),
                pltpu.VMEM((comps, toks, share), BF16),
                pltpu.VMEM((comps, toks, share), BF16),
                pltpu.VMEM((toks, heads), F32),
                pltpu.VMEM((toks, heads), F32),
                pltpu.VMEM((8, heads), F32),
                pltpu.VMEM((toks, 128), F32),
                pltpu.VMEM((toks, toks), BF16),
                pltpu.VMEM((toks, toks), BF16),
                pltpu.VMEM((state + 32, toks), BF16),
                pltpu.VMEM((comps, 8, share), F32),
                pltpu.VMEM((toks, toks), F32),
                pltpu.VMEM((toks, state), F32),
                pltpu.VMEM((toks, 128), F32),
                pltpu.VMEM((2, toks + 8, share), F32),
                pltpu.VMEM((2, toks + 8, share), F32),
                pltpu.VMEM((4, 16, share), F32),
                pltpu.VMEM((4, 16, share), F32),
                pltpu.VMEM((planes, share, state), BF16),
                pltpu.VMEM((planes, 16, share), BF16),
                pltpu.VMEM((comps, share, state), BF16),
                pltpu.VMEM((comps, share, state), BF16),
                pltpu.VMEM((comps, 16, share), BF16),
                pltpu.VMEM((comps, 16, share), BF16),
                pltpu.VMEM((comps, state, share), BF16),
                pltpu.VMEM((comps, state, share), BF16),
                pltpu.VMEM((comps, 16, share), BF16),
                pltpu.VMEM((comps, 16, share), BF16),
                pltpu.VMEM((planes, state + 8, share), F32),
                pltpu.VMEM((planes, state + 8, share), F32),
                pltpu.SemaphoreType.DMA((3,)),
                line,
                line,
                line,
                pair,
                pair,
                pair,
                pair,
            ],
            compiler_params=pltpu.CompilerParams(
                collective_id=0, has_side_effects=True, vmem_limit_bytes=56 << 20
            ),
            cost_estimate=pl.CostEstimate(
                flops=10 * toks * toks * feats,
                bytes_accessed=8 * toks * feats,
                transcendentals=toks * feats,
            ),
            name="mixer",
        )(
            x_in,
            dy_up,
            b_in,
            c_in,
            dt_raw,
            advantages.reshape(1, toks),
            lengths,
            prompt_of.reshape(-1),
            a_log.reshape(1, heads),
            dt_bias.reshape(1, heads),
            skip_gain.reshape(1, heads),
            conv_w,
            conv_b.reshape(1, feats),
            prompt_state.reshape(share, state),
            prompt_tail.reshape(tail_len, share),
        )
        scores, grad_x, grad_state, grad_tail = pl.pallas_call(
            functools.partial(finish, 8),
            out_shape=(
                jax.ShapeDtypeStruct((1, toks), F32),
                jax.ShapeDtypeStruct((toks, feats), BF16),
                jax.ShapeDtypeStruct((share, state), F32),
                jax.ShapeDtypeStruct((tail_len, 1, share), F32),
            ),
            in_specs=[off] * 4,
            out_specs=(off,) * 4,
            scratch_shapes=[
                pltpu.VMEM((1, toks), F32),
                pltpu.VMEM((toks, feats), BF16),
                pltpu.VMEM((share, state), F32),
                pltpu.VMEM((tail_len, 1, share), F32),
                pltpu.SemaphoreType.DMA((2, 11)),
            ],
            compiler_params=pltpu.CompilerParams(vmem_limit_bytes=56 << 20),
            name="finish",
        )(scores, grad_x, grad_state, grad_tail)
        return (
            scores.reshape(toks),
            grad_x,
            grad_state.reshape(prompt_state.shape),
            grad_tail.reshape(tail_len, 1, share).transpose(1, 0, 2),
        )

    return run


def solution(mesh):
    planes, comps = mesh.shape["prompt"], mesh.shape["comp"]
    both = P(("prompt", "comp"))
    rows = P(("prompt", "comp"), None)
    state = P("prompt", "comp", None, None)
    tail = P("prompt", None, "comp")
    in_specs = (rows,) * 5 + (both,) * 2 + (P(),) * 6 + (state, tail)
    out_specs = (both, rows, state, tail)
    return jax.shard_map(
        body(planes, comps), mesh=mesh, in_specs=in_specs, out_specs=out_specs, check_vma=False
    )
```

```python
import functools

import jax
import jax.numpy as jnp
from jax import lax
from jax.experimental import pallas as pl
from jax.experimental.pallas import tpu as pltpu
from jax.sharding import PartitionSpec as P

MESH = pl.DeviceIdType.MESH
F32 = jnp.float32
BF16 = jnp.bfloat16
LN2 = 0.6931471805599453
HIGHEST = lax.Precision.HIGHEST


def split(value):
    high = value.astype(BF16)
    return high, (value - high.astype(F32)).astype(BF16)


def dot(left, right):
    return lax.dot_general(left, right, (((1,), (0,)), ((), ())), preferred_element_type=F32)


def dot_t(left, right):
    return lax.dot_general(left, right, (((1,), (1,)), ((), ())), preferred_element_type=F32)


def offsets(j):
    row = lax.rem(lax.div(j, 4), 4)
    return lax.rem(j, 4), lax.rem(j + row, 4), lax.div(j, 16)


def kernel(
    planes,
    comps,
    x_hbm,
    dy_hbm,
    b_ref,
    c_ref,
    dtr_ref,
    adv_ref,
    len_ref,
    prompt_ref,
    alog_ref,
    dtb_ref,
    skip_ref,
    cw_ref,
    cb_ref,
    st_ref,
    tl_ref,
    score_ref,
    gx_hbm,
    gs_ref,
    gt_ref,
    xv,
    dyv,
    gxv,
    zh,
    zl,
    e1,
    e2,
    scale8,
    wcol,
    mth,
    mtl,
    lead,
    first,
    kacc,
    pacc,
    sacc,
    xs,
    gsc,
    xe,
    ge,
    sall,
    tall,
    ssend,
    srecv,
    tsend,
    trecv,
    gsend,
    grecv,
    hsend,
    hrecv,
    zsend,
    zrecv,
    loc_sem,
    zs_sem,
    zt_sem,
    zg_sem,
    ss_sem,
    ts_sem,
    gsm_sem,
    hs_sem,
):
    toks = b_ref.shape[0]
    heads = alog_ref.shape[1]
    state = b_ref.shape[1]
    width = xv.shape[1] // comps
    z = lax.axis_index("prompt")
    me = lax.axis_index("comp")
    mx, my, mk = lax.div(me, 8), lax.rem(lax.div(me, 2), 4), lax.rem(me, 2)

    def ahead(j):
        ox, oy, ok = offsets(jnp.int32(j))
        return (lax.rem(mx + ox, 4) * 4 + lax.rem(my + oy, 4)) * 2 + lax.rem(mk + ok, 2)

    def behind(j):
        ox, oy, ok = offsets(jnp.int32(j))
        return (lax.rem(mx + 4 - ox, 4) * 4 + lax.rem(my + 4 - oy, 4)) * 2 + lax.rem(mk + ok, 2)

    def plane_copy(src, dst, sems, j, target):
        return pltpu.make_async_remote_copy(
            src_ref=src,
            dst_ref=dst.at[me],
            send_sem=sems.at[0, j],
            recv_sem=sems.at[1, me],
            device_id=(z, target),
            device_id_type=MESH,
        )

    def plane_arrival(src, dst, sems, source):
        return pltpu.make_async_remote_copy(
            src_ref=src,
            dst_ref=dst.at[source],
            send_sem=sems.at[0, 0],
            recv_sem=sems.at[1, source],
            device_id=(z, source),
            device_id_type=MESH,
        )

    def line_copy(src, dst, sems, step):
        return pltpu.make_async_remote_copy(
            src_ref=src,
            dst_ref=dst.at[z],
            send_sem=sems.at[0, step],
            recv_sem=sems.at[1, z],
            device_id=((z + step) % planes, me),
            device_id_type=MESH,
        )

    def line_arrival(src, dst, sems, step):
        source = (z + planes - step) % planes
        return pltpu.make_async_remote_copy(
            src_ref=src,
            dst_ref=dst.at[source],
            send_sem=sems.at[0, step],
            recv_sem=sems.at[1, source],
            device_id=(source, me),
            device_id_type=MESH,
        )

    load_dy = pltpu.make_async_copy(dy_hbm, dyv, loc_sem.at[0])
    load_x = pltpu.make_async_copy(x_hbm, xv, loc_sem.at[1])
    load_dy.start()
    load_x.start()

    barrier = pltpu.get_barrier_semaphore()

    def greet(j, carry):
        pl.semaphore_signal(barrier, inc=1, device_id=(z, ahead(j)), device_id_type=MESH)
        return carry

    lax.fori_loop(1, comps, greet, 0)
    for step in range(1, planes):
        pl.semaphore_signal(
            barrier, inc=1, device_id=((z + step) % planes, me), device_id_type=MESH
        )

    sall[z] = st_ref[...].astype(BF16)
    xe[0] = jnp.zeros((16, width), F32)
    xe[0, 5:8, :] = tl_ref[...].astype(F32)
    tall[z] = xe[0].astype(BF16)

    row = lax.broadcasted_iota(jnp.int32, (toks, toks), 0)
    col = lax.broadcasted_iota(jnp.int32, (toks, toks), 1)
    raw = dtr_ref[...] + dtb_ref[...]
    dt = jnp.maximum(raw, 0.0) + jnp.log1p(jnp.exp(-jnp.abs(raw)))
    total = lax.dot_general(
        jnp.where(row >= col, 1.0, 0.0),
        dt * jnp.exp(alog_ref[...]),
        (((1,), (0,)), ((), ())),
        precision=HIGHEST,
        preferred_element_type=F32,
    )
    power = jnp.floor(total[toks // 2 - 1 : toks // 2, :] * (1.0 / LN2) + 0.5)
    offset = total - power * LN2
    e1[...] = jnp.exp(-offset)
    e2[...] = dt * jnp.exp(offset)
    scale8[...] = jnp.broadcast_to(jnp.exp2(-power), (8, heads))
    weight = jnp.where(
        lax.broadcasted_iota(jnp.int32, (1, toks), 1) < len_ref[...],
        adv_ref[...].astype(F32) / 1024.0,
        0.0,
    )
    wcol[...] = jnp.broadcast_to(
        jnp.sum(jnp.where(row == col, weight, 0.0), axis=1, keepdims=True), (toks, 128)
    )
    high, low = split(jnp.where(row <= col, dot_t(b_ref[...], c_ref[...]), 0.0))
    mth[...] = high
    mtl[...] = low
    lead[0:state, :] = jnp.transpose(c_ref[...].astype(F32)).astype(BF16)
    lead[state : state + 16, :] = high[0:16, :]
    lead[state + 16 :, :] = low[0:16, :]
    kacc[...] = jnp.zeros_like(kacc)
    pacc[...] = jnp.zeros_like(pacc)
    sacc[...] = jnp.zeros_like(sacc)
    for u in range(2):
        gsc[u, toks:, :] = jnp.zeros((8, width), F32)

    pl.semaphore_wait(barrier, comps - 1 + planes - 1)
    for step in range(1, planes):
        line_copy(tall.at[z], tall, zt_sem, step).start()
    for step in range(1, planes):
        line_copy(sall.at[z], sall, zs_sem, step).start()

    half = lax.broadcasted_iota(jnp.int32, (toks, 128), 1) // 64
    half8 = lax.broadcasted_iota(jnp.int32, (8, 128), 1) // 64
    group = width // 64

    def spread(value, index, block):
        parts = [
            jnp.take_along_axis(value, index + (block * group + 2 * i), axis=1)
            for i in range(width // 128)
        ]
        return jnp.concatenate(parts, axis=1)

    def lanes(value):
        return jnp.concatenate([value] * (width // 128), axis=1)

    load_dy.wait()

    def readout(i, carry):
        for u in range(4):
            j = 4 * i + u
            target = ahead(j)
            cols = pl.ds(pl.multiple_of(target * width, width), width)
            zval = spread(e1[...], half, target) * (lanes(wcol[...]) * dyv[:, cols].astype(F32))
            zhigh, zlow = split(zval)
            zh[target] = zhigh
            zl[target] = zlow
            part = dot(lead[...], zhigh) + dot(lead[...], zlow)
            scale = spread(scale8[...], half8, target)[0:1, :]
            gsend[j] = (part[0:state, :] * scale).astype(BF16)
            first[target] = part[state : state + 8, :] + part[state + 16 : state + 24, :]
        for u in range(4):
            j = 4 * i + u

            def send():
                plane_copy(gsend.at[j], grecv, gsm_sem, j, ahead(j)).start()

            if u:
                send()
            else:
                pl.when(i > 0)(send)
        return carry

    lax.fori_loop(0, 2, readout, 0)

    for step in range(1, planes):
        line_arrival(tall.at[z], tall, zt_sem, step).wait_recv()

    def send_tail(j, carry):
        target = ahead(j)
        tsend[j] = tall[prompt_ref[z * comps + target]]
        plane_copy(tsend.at[j], trecv, ts_sem, j, target).start()
        return carry

    lax.fori_loop(1, comps, send_tail, 0)
    trecv[me] = tall[prompt_ref[z * comps + me]]
    lax.fori_loop(2, comps // 4, readout, 0)
    grecv[me] = gsend[0]

    load_x.wait()
    skip8 = jnp.broadcast_to(skip_ref[...], (8, heads))

    def arrive_tail(j, carry):
        plane_arrival(tsend.at[0], trecv, ts_sem, lax.rem(me + j, comps)).wait_recv()
        return carry

    lax.fori_loop(1, comps, arrive_tail, 0)

    def gate(conv):
        rise = jnp.tanh(conv) + 1.0
        act = conv * rise
        return act, rise + act * (2.0 - rise)

    def edge(i, carry):
        for u in range(4):
            j = 4 * i + u
            block = ahead(j)
            cols = pl.ds(pl.multiple_of(block * width, width), width)
            xe[u, 0:8, :] = trecv[block].astype(F32)[0:8, :]
            xe[u, 8:16, :] = xv[0:16, cols].astype(F32)[0:8, :]
            taps = 0.5 * cw_ref[:, cols]
            conv = 0.5 * cb_ref[:, cols] + taps[3:4] * xe[u, 8:16, :]
            for k in range(3):
                conv = conv + taps[k : k + 1] * xe[u, 5 + k : 13 + k, :]
            slope = gate(conv)[1]
            direct = spread(skip8, half8, block) * (
                lanes(wcol[0:8, :]) * dyv[0:16, cols].astype(F32)[0:8, :]
            )
            ge[u, 0:8, :] = jnp.zeros((8, width), F32)
            ge[u, 8:16, :] = (spread(e2[0:8, :], half8, block) * first[block] + direct) * slope
            grad = taps[3:4] * ge[u, 0:8, :]
            for k in range(3):
                grad = grad + taps[k : k + 1] * ge[u, 3 - k : 11 - k, :]
            high = grad.astype(BF16).astype(F32)
            hsend[j] = jnp.concatenate([high, grad - high], axis=0).astype(BF16)
        for u in range(4):
            j = 4 * i + u

            def send():
                plane_copy(hsend.at[j], hrecv, hs_sem, j, ahead(j)).start()

            if u:
                send()
            else:
                pl.when(i > 0)(send)
        return carry

    lax.fori_loop(0, comps // 4, edge, 0)
    hrecv[me] = hsend[0]

    for step in range(1, planes):
        line_arrival(sall.at[z], sall, zs_sem, step).wait_recv()

    def send_state(j, carry):
        target = ahead(j)
        ssend[j] = sall[prompt_ref[z * comps + target]]
        plane_copy(ssend.at[j], srecv, ss_sem, j, target).start()
        return carry

    lax.fori_loop(1, comps, send_state, 0)
    srecv[me] = sall[prompt_ref[z * comps + me]]

    def mix(i, carry):
        for u in range(2):
            block = 2 * i + u
            cols = pl.ds(pl.multiple_of(block * width, width), width)
            xs[u, 0:8, :] = trecv[block].astype(F32)[0:8, :]
            xs[u, 8:, :] = xv[:, cols].astype(F32)
            taps = 0.5 * cw_ref[:, cols]
            conv = 0.5 * cb_ref[:, cols] + taps[3:4] * xs[u, 8:, :]
            for k in range(3):
                conv = conv + taps[k : k + 1] * xs[u, 5 + k : 5 + k + toks, :]
            act, slope = gate(conv)
            late = spread(e2[...], half, block)
            vhigh, vlow = split(late * act)
            zhigh, zlow = zh[block], zl[block]
            kacc[...] += dot_t(zhigh, vhigh) + dot_t(zlow, vhigh) + dot_t(zhigh, vlow)
            back = dot(mth[...], zhigh) + dot(mth[...], zlow) + dot(mtl[...], zhigh)
            direct = spread(skip8, half8, block)[0:1, :] * (
                lanes(wcol[...]) * dyv[:, cols].astype(F32)
            )
            seen = act * direct
            sacc[...] += seen[:, :128] + seen[:, 128:]
            gsc[u, 0:toks, :] = (late * back + direct) * slope
            grad = taps[3:4] * gsc[u, 0:toks, :]
            for k in range(3):
                grad = grad + taps[k : k + 1] * gsc[u, 3 - k : 3 - k + toks, :]
            gxv[:, cols] = grad.astype(BF16)
        return carry

    lax.fori_loop(0, comps // 2, mix, 0)
    store_gx = pltpu.make_async_copy(gxv, gx_hbm, loc_sem.at[2])
    store_gx.start()

    def arrive(j, carry):
        source = lax.rem(me + j, comps)
        plane_arrival(gsend.at[0], grecv, gsm_sem, source).wait_recv()
        plane_arrival(hsend.at[0], hrecv, hs_sem, source).wait_recv()
        return carry

    lax.fori_loop(1, comps, arrive, 0)

    def gather(r, carry):
        rows = pl.ds(pl.multiple_of(r * 16, 16), 16)
        sums = [jnp.zeros((16, width), F32) for _ in range(planes)]
        for source in range(comps):
            held = prompt_ref[z * comps + source]
            term = grecv[source, rows, :].astype(F32)
            sums = [sums[q] + jnp.where(held == q, term, 0.0) for q in range(planes)]
        for q in range(planes):
            zsend[q, rows, :] = sums[q]
        return carry

    lax.fori_loop(0, state // 16, gather, 0)
    sums = [jnp.zeros((8, width), F32) for _ in range(planes)]
    for source in range(comps):
        held = prompt_ref[z * comps + source]
        term = hrecv[source].astype(F32)
        term = term[0:8, :] + term[8:16, :]
        sums = [sums[q] + jnp.where(held == q, term, 0.0) for q in range(planes)]
    for q in range(planes):
        zsend[q, state:, :] = sums[q]
    for step in range(1, planes):
        line_copy(zsend.at[(z + step) % planes], zrecv, zg_sem, step).start()
    zrecv[z] = zsend[z]

    beside = lax.rem(me + 1, comps)

    def leave(j, carry):
        plane_copy(tsend.at[j], trecv, ts_sem, j, beside).wait_send()
        plane_copy(gsend.at[j], grecv, gsm_sem, j, beside).wait_send()
        plane_copy(hsend.at[j], hrecv, hs_sem, j, beside).wait_send()
        return carry

    lax.fori_loop(1, comps, leave, 0)

    def prefix(i, carry):
        for u in range(4):
            j = 4 * i + u

            def arrive_state():
                plane_arrival(ssend.at[0], srecv, ss_sem, behind(j)).wait_recv()

            if u:
                arrive_state()
            else:
                pl.when(i > 0)(arrive_state)
        total = pacc[...]
        for u in range(4):
            block = behind(4 * i + u)
            scales = [
                jnp.take_along_axis(
                    scale8[...], jnp.full((8, 128), block * group + g, jnp.int32), axis=1
                )[0:1, :]
                for g in range(group)
            ]
            states = jnp.concatenate(
                [
                    srecv[block, 64 * g : 64 * g + 64, :].astype(F32) * scales[g]
                    for g in range(group)
                ],
                axis=0,
            ).astype(BF16)
            total = total + dot(zh[block], states) + dot(zl[block], states)
        pacc[...] = total
        return carry

    lax.fori_loop(0, comps // 4, prefix, 0)
    aff = dot_t(c_ref[...], b_ref[...])
    scores = (
        jnp.sum(jnp.where(row >= col, aff * kacc[...], 0.0), axis=1, keepdims=True)
        + jnp.sum(sacc[...], axis=1, keepdims=True)
        + jnp.sum(pacc[...] * c_ref[...].astype(F32), axis=1, keepdims=True)
    )
    score_ref[...] = jnp.sum(jnp.where(row == col, scores, 0.0), axis=0, keepdims=True)

    def leave_state(j, carry):
        plane_copy(ssend.at[j], srecv, ss_sem, j, beside).wait_send()
        return carry

    lax.fori_loop(1, comps, leave_state, 0)
    for step in range(1, planes):
        line_copy(tall.at[z], tall, zt_sem, step).wait_send()
        line_copy(sall.at[z], sall, zs_sem, step).wait_send()
    for step in range(1, planes):
        line_arrival(zsend.at[0], zrecv, zg_sem, step).wait_recv()
    whole = zrecv[0] + zrecv[1]
    for q in range(2, planes):
        whole = whole + zrecv[q]
    gs_ref[...] = jnp.transpose(whole[0:state, :])
    gt_ref[...] = whole[state + 5 : state + 8, :].reshape(gt_ref.shape)
    for step in range(1, planes):
        line_copy(zsend.at[(z + step) % planes], zrecv, zg_sem, step).wait_send()
    store_gx.wait()


def finish(parts, *refs):
    sources, targets, held, sems = refs[0:4], refs[4:8], refs[8:12], refs[12]
    rows = held[1].shape[0] // parts
    spans = [(1, pl.ds(rows * i, rows)) for i in range(parts)] + [
        (i, pl.ds(0, held[i].shape[0])) for i in (0, 2, 3)
    ]
    loads = [
        pltpu.make_async_copy(sources[i].at[span], held[i].at[span], sems.at[0, n])
        for n, (i, span) in enumerate(spans)
    ]
    stores = [
        pltpu.make_async_copy(held[i].at[span], targets[i].at[span], sems.at[1, n])
        for n, (i, span) in enumerate(spans)
    ]
    for load in loads:
        load.start()
    for load, store in zip(loads, stores):
        load.wait()
        store.start()
    for store in stores:
        store.wait()


def body(planes, comps):
    def run(
        x_in,
        b_in,
        c_in,
        dt_raw,
        dy_up,
        advantages,
        lengths,
        prompt_of,
        a_log,
        dt_bias,
        skip_gain,
        conv_w,
        conv_b,
        prompt_state,
        prompt_tail,
    ):
        toks, feats = x_in.shape
        heads = a_log.shape[0]
        state = b_in.shape[1]
        share = feats // comps
        tail_len = prompt_tail.shape[1]
        vmem = pl.BlockSpec(memory_space=pltpu.VMEM)
        smem = pl.BlockSpec(memory_space=pltpu.SMEM)
        off = pl.BlockSpec(memory_space=pltpu.HBM)
        hbm = pl.BlockSpec(memory_space=pl.ANY)
        pair = pltpu.SemaphoreType.DMA((2, comps))
        line = pltpu.SemaphoreType.DMA((2, planes))
        scores, grad_x, grad_state, grad_tail = pl.pallas_call(
            functools.partial(kernel, planes, comps),
            out_shape=(
                jax.ShapeDtypeStruct((1, toks), F32),
                jax.ShapeDtypeStruct((toks, feats), BF16),
                jax.ShapeDtypeStruct((share, state), F32),
                jax.ShapeDtypeStruct((tail_len, 1, share), F32),
            ),
            in_specs=[off, off, vmem, vmem, vmem, vmem, vmem, smem] + [vmem] * 7,
            out_specs=(vmem, hbm, vmem, vmem),
            scratch_shapes=[
                pltpu.VMEM((toks, feats), BF16),
                pltpu.VMEM((toks, feats), BF16),
                pltpu.VMEM((toks, feats), BF16),
                pltpu.VMEM((comps, toks, share), BF16),
                pltpu.VMEM((comps, toks, share), BF16),
                pltpu.VMEM((toks, heads), F32),
                pltpu.VMEM((toks, heads), F32),
                pltpu.VMEM((8, heads), F32),
                pltpu.VMEM((toks, 128), F32),
                pltpu.VMEM((toks, toks), BF16),
                pltpu.VMEM((toks, toks), BF16),
                pltpu.VMEM((state + 32, toks), BF16),
                pltpu.VMEM((comps, 8, share), F32),
                pltpu.VMEM((toks, toks), F32),
                pltpu.VMEM((toks, state), F32),
                pltpu.VMEM((toks, 128), F32),
                pltpu.VMEM((2, toks + 8, share), F32),
                pltpu.VMEM((2, toks + 8, share), F32),
                pltpu.VMEM((4, 16, share), F32),
                pltpu.VMEM((4, 16, share), F32),
                pltpu.VMEM((planes, share, state), BF16),
                pltpu.VMEM((planes, 16, share), BF16),
                pltpu.VMEM((comps, share, state), BF16),
                pltpu.VMEM((comps, share, state), BF16),
                pltpu.VMEM((comps, 16, share), BF16),
                pltpu.VMEM((comps, 16, share), BF16),
                pltpu.VMEM((comps, state, share), BF16),
                pltpu.VMEM((comps, state, share), BF16),
                pltpu.VMEM((comps, 16, share), BF16),
                pltpu.VMEM((comps, 16, share), BF16),
                pltpu.VMEM((planes, state + 8, share), F32),
                pltpu.VMEM((planes, state + 8, share), F32),
                pltpu.SemaphoreType.DMA((3,)),
                line,
                line,
                line,
                pair,
                pair,
                pair,
                pair,
            ],
            compiler_params=pltpu.CompilerParams(
                collective_id=0, has_side_effects=True, vmem_limit_bytes=56 << 20
            ),
            cost_estimate=pl.CostEstimate(
                flops=10 * toks * toks * feats,
                bytes_accessed=8 * toks * feats,
                transcendentals=toks * feats,
            ),
            name="mixer",
        )(
            x_in,
            dy_up,
            b_in,
            c_in,
            dt_raw,
            advantages.reshape(1, toks),
            lengths.reshape(1, 1),
            prompt_of.reshape(-1),
            a_log.reshape(1, heads),
            dt_bias.reshape(1, heads),
            skip_gain.reshape(1, heads),
            conv_w,
            conv_b.reshape(1, feats),
            prompt_state.reshape(share, state),
            prompt_tail.reshape(tail_len, share),
        )
        scores, grad_x, grad_state, grad_tail = pl.pallas_call(
            functools.partial(finish, 8),
            out_shape=(
                jax.ShapeDtypeStruct((1, toks), F32),
                jax.ShapeDtypeStruct((toks, feats), BF16),
                jax.ShapeDtypeStruct((share, state), F32),
                jax.ShapeDtypeStruct((tail_len, 1, share), F32),
            ),
            in_specs=[off] * 4,
            out_specs=(off,) * 4,
            scratch_shapes=[
                pltpu.VMEM((1, toks), F32),
                pltpu.VMEM((toks, feats), BF16),
                pltpu.VMEM((share, state), F32),
                pltpu.VMEM((tail_len, 1, share), F32),
                pltpu.SemaphoreType.DMA((2, 11)),
            ],
            compiler_params=pltpu.CompilerParams(vmem_limit_bytes=56 << 20),
            name="finish",
        )(scores, grad_x, grad_state, grad_tail)
        return (
            scores.reshape(toks),
            grad_x,
            grad_state.reshape(prompt_state.shape),
            grad_tail.reshape(tail_len, 1, share).transpose(1, 0, 2),
        )

    return run


def solution(mesh):
    planes, comps = mesh.shape["prompt"], mesh.shape["comp"]
    both = P(("prompt", "comp"))
    rows = P(("prompt", "comp"), None)
    state = P("prompt", "comp", None, None)
    tail = P("prompt", None, "comp")
    in_specs = (rows,) * 5 + (both,) * 2 + (P(),) * 6 + (state, tail)
    out_specs = (both, rows, state, tail)
    return jax.shard_map(
        body(planes, comps), mesh=mesh, in_specs=in_specs, out_specs=out_specs, check_vma=False
    )
```
